256 devices in a mesh: tm: 4 (over y), height: 4 (over x), width: 16 (over z, core).
Axes of the slice: x: 4, y: 4, z: 8, core: 2. Of those that a mesh axis runs over, the one named last changes fastest.
Arguments:
- features: bfloat16 [16, 32, 160, 384], P('tm', 'height', 'width'), may hold values from -6 to 6
- first_gain: float32 [384], replicated, may hold values from 0.5 to 2
- first_kernel: bfloat16 [27, 384, 384], P(None, ('height', 'width')), may hold values from -0.0625 to 0.0625
- first_bias: float32 [384], replicated, may hold values from -3 to 3
- second_gain: float32 [384], replicated, may hold values from 0.5 to 2
- second_kernel: bfloat16 [27, 384, 384], P(None, ('height', 'width')), may hold values from -0.0625 to 0.0625
- second_bias: float32 [384], replicated, may hold values from -3 to 3
Outputs:
- block_out: bfloat16 [16, 32, 160, 384], P('tm', 'height', 'width')
The draws below stay inside these ranges and needn't reach their ends.
All inputs are finite; a program needn't handle non-finite values.
Results may differ from the reference program's by a relative error of at most 0.012.
Values may be sent and summed in bfloat16 or wider, within the bound.
No kernel may reach another device: no remote copies, remote signals or barrier semaphores. Data moves between devices by JAX's collectives and lax.ppermute only.
A program may use at most 128 MiB of HBM per device.

```python
import math
import jax
import jax.numpy as jnp
from jax import lax

CH = 384
TAPS = 27
NT = 16
NH = 32
NW = 160


def levels(stream_key, shape, shards, smallest, largest):
    factor_of, own = 1.0, jax.random.fold_in(stream_key, 6)
    for position, blocks in shards:
        draws = jnp.exp(jax.random.uniform(jax.random.fold_in(own, position), (blocks,), jnp.float32, smallest / len(shards), largest / len(shards)))
        factor_of = factor_of * jnp.repeat(draws, shape[position] // blocks).reshape([-1 if axis == position else 1 for axis in range(len(shape))])
    return factor_of


def noise(own_key, extent, scale, most, shards=(), held_as=jnp.bfloat16):
    values = jax.random.normal(own_key, extent, jnp.float32) * scale
    if len(shards) > 0:
        values = levels(own_key, extent, shards, -0.22, 0.18) * values
    return jnp.clip(values, min=-most, max=most).astype(held_as)


def setup_inputs(seed: int = 0) -> dict:
    seeds = jax.random.split(jax.random.key(seed), 8)
    features = noise(seeds[0], (NT, NH, NW, CH), 1.0, 6.0, ((0, 4), (1, 4), (2, 16)))
    first_gain = jnp.clip(jnp.exp(jax.random.uniform(seeds[1], (CH,), jnp.float32, math.log(0.5), math.log(2.0))), 0.5, 2.0)
    first_kernel = noise(seeds[2], (TAPS, CH, CH), (TAPS * CH) ** -0.5, 0.0625, ((1, 64),))
    first_bias = noise(seeds[3], (CH,), 0.5, 3.0, (), jnp.float32)
    second_gain = jnp.clip(jnp.exp(jax.random.uniform(seeds[4], (CH,), jnp.float32, math.log(0.5), math.log(2.0))), 0.5, 2.0)
    second_kernel = noise(seeds[5], (TAPS, CH, CH), (TAPS * CH) ** -0.5, 0.0625, ((1, 64),))
    second_bias = noise(seeds[6], (CH,), 0.5, 3.0, (), jnp.float32)
    return {"features": features, "first_gain": first_gain, "first_kernel": first_kernel, "first_bias": first_bias, "second_gain": second_gain, "second_kernel": second_kernel, "second_bias": second_bias}


def activate(volume, gain):
    values = volume.astype(jnp.float32)
    square_mean = lax.optimization_barrier(jnp.mean(values * values, axis=-1, keepdims=True))
    normed = values * lax.rsqrt(square_mean + 1e-06) * gain
    return jax.nn.silu(normed).astype(jnp.bfloat16)

def convolve(active, kernel, bias):
    frames, rows, cols, chans = active.shape
    padded = jnp.pad(active.astype(jnp.float32), ((2, 0), (1, 1), (1, 1), (0, 0)))
    total = jnp.zeros((frames * rows * cols, kernel.shape[2]), jnp.float32)
    for step_t in range(3):
        for step_h in range(3):
            for step_w in range(3):
                window = padded[step_t:step_t + frames, step_h:step_h + rows, step_w:step_w + cols]
                tap_kernel = kernel[9 * step_t + 3 * step_h + step_w].astype(jnp.float32)
                total = total + jnp.dot(window.reshape(-1, chans), tap_kernel, precision=lax.Precision.HIGHEST)
    return total.reshape(frames, rows, cols, kernel.shape[2]) + bias

def reference(features, first_gain, first_kernel, first_bias, second_gain, second_kernel, second_bias):
    first_active = activate(features, first_gain)
    middle = convolve(first_active, first_kernel, first_bias).astype(jnp.bfloat16)
    second_active = activate(middle, second_gain)
    summed = convolve(second_active, second_kernel, second_bias) + features.astype(jnp.float32)
    return summed.astype(jnp.bfloat16)
```

```python
import jax
import jax.numpy as jnp
from jax import lax
from jax.experimental import pallas as pl
from jax.experimental.pallas import tpu as pltpu
from jax.sharding import Mesh, PartitionSpec as P

AXES = ("t", "h", "z", "c")
SHIFT = ((0, 4), (1, -3), (-1, 3), (2, -2))
MAIN = tuple(t for t in range(27) if t % 3 != 1)
PAIRED = (1, 4, 7, 10, 13, 16)
ALONE = (19, 22, 25)
GROUPS = len(MAIN) + len(ALONE)
CHANS = 384
LANES = 256
WIDE = 32
BF = jnp.bfloat16
F32 = jnp.float32
VMEM = pltpu.CompilerParams(vmem_limit_bytes=56 * 2**20)
whole = pl.BlockSpec(memory_space=pltpu.VMEM)
scalars = pl.BlockSpec(memory_space=pltpu.SMEM)


def move(x, sizes, source):
    def place(at):
        index = 0
        for coordinate, size in zip(at, sizes):
            index = index * size + coordinate % size
        return index

    pairs = []
    for index in range(sizes[0] * sizes[1] * sizes[2] * sizes[3]):
        rest, c = divmod(index, sizes[3])
        rest, z = divmod(rest, sizes[2])
        t, h = divmod(rest, sizes[1])
        at = source(t, h, z, c)
        if at is not None:
            pairs.append((place(at), index))
    return lax.ppermute(x, AXES, pairs)


def fold_kernel(k_ref, out_ref):
    for g in range(GROUPS):
        if g < len(MAIN):
            low = k_ref[MAIN[g]].astype(F32)
            k = 2 * (g % 3)
            high = k_ref[PAIRED[g // 3]].astype(F32)[k : k + 2]
        else:
            low = k_ref[ALONE[g - len(MAIN)]].astype(F32)
            high = jnp.zeros((2, CHANS), F32)
        out_ref[g] = jnp.concatenate([low, high], axis=0).astype(BF)


def fold(kernel):
    return pl.pallas_call(
        fold_kernel,
        out_shape=jax.ShapeDtypeStruct((GROUPS, 8, CHANS), BF),
        in_specs=[whole],
        out_specs=whole,
        name="fold",
    )(kernel)


def spread(place_ref):
    t, h, z, c = (place_ref[0], place_ref[1], place_ref[2], place_ref[3])
    lane = lax.broadcasted_iota(jnp.int32, (1, LANES), 1)
    j = lane & 7
    p = lane >> 3
    outer, inner, far = p >> 3, (p >> 1) & 3, p & 1
    t_of = (t + jnp.where(c == 0, inner, outer)) & 3
    h_of = (h + jnp.where(c == 0, outer, inner)) & 3
    shift = jnp.where(t_of == 0, 0, jnp.where(t_of == 1, 1, jnp.where(t_of == 2, 7, 2)))
    z_of = (z + shift + 4 * far) & 7
    base = 96 * h_of + 12 * z_of + 6 * c
    chan = lax.broadcasted_iota(jnp.int32, (CHANS, LANES), 0)
    matrices = [jnp.where(chan == jnp.where(j < 6, base + j, -1), 1.0, 0.0)]
    for k in range(3):
        wanted = jnp.where(j >= 6, base + 2 * k + j - 6, -1)
        matrices.append(jnp.where(chan == wanted, 1.0, 0.0))
    return [m.astype(BF) for m in matrices]


def activated(values, gain):
    square_mean = jnp.mean(values * values, axis=-1, keepdims=True)
    normed = values * lax.rsqrt(square_mean + 1e-06) * gain
    return normed * jax.nn.sigmoid(normed)


def lay_out(active, rows, place_ref, out_ref):
    p0, p1, p2, p3 = spread(place_ref)
    count = rows * 24

    def put(slot, value, matrix):
        laid = jnp.dot(value, matrix, preferred_element_type=F32).astype(BF)
        out_ref[slot, 0, :, 0:24, :] = laid.reshape(rows, 24, LANES)

    put(0, active.astype(BF), p0)
    one = pltpu.roll(active, count - 1, 0).astype(BF)
    put(1, one, p0)
    put(3, one, p1)
    put(4, one, p2)
    put(5, one, p3)
    put(2, pltpu.roll(active, count - 2, 0).astype(BF), p0)


def first_layout_kernel(place_ref, x_ref, gain_ref, out_ref):
    values = x_ref[0].astype(F32).reshape(12 * 24, CHANS)
    lay_out(activated(values, gain_ref[...]), 12, place_ref, out_ref)


def first_layout(place, features, gain):
    return pl.pallas_call(
        first_layout_kernel,
        grid=(8,),
        out_shape=jax.ShapeDtypeStruct((6, 8, 12, WIDE, LANES), BF),
        in_specs=[
            scalars,
            pl.BlockSpec((1, 12, 24, CHANS), lambda f: (f, 0, 0, 0)),
            pl.BlockSpec((1, CHANS), lambda f: (0, 0)),
        ],
        out_specs=pl.BlockSpec((6, 1, 12, WIDE, LANES), lambda f: (0, f, 0, 0, 0)),
        compiler_params=VMEM,
        name="first_layout",
    )(place, features, gain)


def second_layout_kernel(place_ref, mine_ref, other_ref, bias_ref, gain_ref, out_ref):
    frame = pl.program_id(0) - 2 + 4 * place_ref[0]
    total = mine_ref[0] + other_ref[0].astype(F32)
    total = total.reshape(10 * 24, CHANS) + bias_ref[...]
    active = activated(total.astype(BF).astype(F32), gain_ref[...])
    index = lax.broadcasted_iota(jnp.int32, (10, 24, 1), 0)
    row = index + 8 * place_ref[1] - 1
    col = lax.broadcasted_iota(jnp.int32, (10, 24, 1), 1) + 20 * place_ref[2] - 1
    inside = (row >= 0) & (row < 32) & (col >= 0) & (col < 160) & (frame >= 0)
    keep = jnp.where(inside, 1.0, 0.0)
    active = (active.reshape(10, 24, CHANS) * keep).reshape(10 * 24, CHANS)
    lay_out(active, 10, place_ref, out_ref)


def second_layout(place, mine, other, bias, gain):
    return pl.pallas_call(
        second_layout_kernel,
        grid=(6,),
        out_shape=jax.ShapeDtypeStruct((6, 6, 10, WIDE, LANES), BF),
        in_specs=[
            scalars,
            pl.BlockSpec((1, 10, 24, CHANS), lambda f: (f, 0, 0, 0)),
            pl.BlockSpec((1, 10, 24, CHANS), lambda f: (f, 0, 0, 0)),
            pl.BlockSpec((1, CHANS), lambda f: (0, 0)),
            pl.BlockSpec((1, CHANS), lambda f: (0, 0)),
        ],
        out_specs=pl.BlockSpec((6, 1, 10, WIDE, LANES), lambda f: (0, f, 0, 0, 0)),
        compiler_params=VMEM,
        name="second_layout",
    )(place, mine, other, bias, gain)


def tap_sum(laid_ref, blocks, first, frames, rows):
    def window(slot, tap):
        dt, dh = tap // 9, tap % 9 // 3
        at = pl.ds(first + dt, frames)
        return laid_ref[slot, at, dh : dh + rows].reshape(-1, LANES)

    total = jnp.zeros((frames * rows * WIDE, CHANS), F32)
    for g in range(GROUPS):
        if g < len(MAIN):
            left = window(MAIN[g] % 3, MAIN[g]) + window(3 + g % 3, PAIRED[g // 3])
        else:
            left = window(1, ALONE[g - len(MAIN)])
        right = jnp.concatenate([b[i, g] for b in blocks for i in range(b.shape[0])], axis=0)
        total = total + jnp.dot(left, right, preferred_element_type=F32)
    return total.reshape(frames, rows, WIDE, CHANS)


def first_conv_kernel(laid_ref, b0, b1, b2, b3, b4, mine_ref, sent_ref):
    step = pl.program_id(0)
    total = tap_sum(laid_ref, (b0, b1, b2, b3, b4), 2 * step, 2, 10)[:, :, 0:24]
    mine_ref[...] = total
    sent_ref[...] = total.astype(BF)


def first_conv(laid, blocks):
    out = pl.BlockSpec((2, 10, 24, CHANS), lambda f: (f, 0, 0, 0))
    return pl.pallas_call(
        first_conv_kernel,
        grid=(3,),
        out_shape=(
            jax.ShapeDtypeStruct((6, 10, 24, CHANS), F32),
            jax.ShapeDtypeStruct((6, 10, 24, CHANS), BF),
        ),
        in_specs=[whole] * 6,
        out_specs=(out, out),
        compiler_params=VMEM,
        name="first_conv",
    )(laid, *blocks)


def second_conv_kernel(place_ref, laid_ref, b0, b1, b2, b3, b4, mine_ref, sent_ref):
    step = pl.program_id(0)
    total = tap_sum(laid_ref, (b0, b1, b2, b3, b4), 2 * step, 2, 8)
    left, right = total[:, :, 0:10], total[:, :, 10:20]
    low = place_ref[3] == 0
    mine_ref[...] = jnp.where(low, left, right)
    sent_ref[...] = jnp.where(low, right, left)


def second_conv(place, laid, blocks):
    out = pl.BlockSpec((2, 8, 10, CHANS), lambda f: (f, 0, 0, 0))
    return pl.pallas_call(
        second_conv_kernel,
        grid=(2,),
        out_shape=(
            jax.ShapeDtypeStruct((4, 8, 10, CHANS), F32),
            jax.ShapeDtypeStruct((4, 8, 10, CHANS), F32),
        ),
        in_specs=[scalars] + [whole] * 6,
        out_specs=(out, out),
        compiler_params=VMEM,
        name="second_conv",
    )(place, laid, *blocks)


def solution(mesh):
    sizes = (mesh.shape["tm"], mesh.shape["height"], mesh.shape["width"] // 2, 2)
    split = Mesh(mesh.devices.reshape(sizes), AXES)

    def sent(x, source):
        return move(x, sizes, source)

    def along(first, step):
        def source(t, h, z, c):
            return (t + step, h, z, c) if (c == 0) == first else (t, h + step, z, c)

        return source

    def z_stage(x):
        near = sent(x, lambda t, h, z, c: (t, h, z + SHIFT[t][0], c))
        far = sent(x, lambda t, h, z, c: (t, h, z + SHIFT[t][1], c))
        return jnp.concatenate([near, far], axis=1)

    def first_ring(x):
        up, down = sent(x, along(True, 1)), sent(x, along(True, -1))
        return jnp.stack([x, up, sent(x, along(True, 2)), down])

    def second_ring(x):
        up, down = sent(x, along(False, 1)), sent(x, along(False, -1))
        half = sent(up[:2], along(False, 1))
        other = sent(down[2:], along(False, -1))
        return x, up, half, other, down

    def swapped(x):
        return sent(x, lambda t, h, z, c: (t, h, z, 1 - c))

    def inner(at, d):
        return at if all(0 <= a < s for a, s in zip(at, sizes)) else None

    def widened(x, core):
        earlier = sent(x, lambda t, h, z, c: inner((t - 1, h, z, c), 0))
        x = jnp.concatenate([earlier, x], axis=0)
        above = sent(x[:, -2:], lambda t, h, z, c: inner((t, h - 1, z, c), 0))
        below = sent(x[:, :2], lambda t, h, z, c: inner((t, h + 1, z, c), 0))
        x = jnp.concatenate([above, x, below], axis=1)
        edge = jnp.where(core == 0, x[:, :, :2], x[:, :, -2:])
        beside = sent(edge, lambda t, h, z, c: inner((t, h, z + 2 * c - 1, 1 - c), 0))
        mine = jnp.where(
            core == 0,
            jnp.concatenate([beside, x], axis=2),
            jnp.concatenate([x, beside], axis=2),
        )
        other = swapped(mine)
        return jnp.where(
            core == 0,
            jnp.concatenate([mine, other], axis=2),
            jnp.concatenate([other, mine], axis=2),
        )

    def on_device(features, gain_1, kernel_1, bias_1, gain_2, kernel_2, bias_2):
        place = jnp.stack([lax.axis_index(a) for a in AXES]).astype(jnp.int32)
        core = lax.axis_index("c")
        one = first_ring(z_stage(fold(kernel_1)))
        two = first_ring(z_stage(fold(kernel_2)))
        laid = first_layout(place, widened(features, core), gain_1.reshape(1, CHANS))
        mine, passed = first_conv(laid, second_ring(one))
        laid = second_layout(
            place, mine, swapped(passed), bias_1.reshape(1, CHANS), gain_2.reshape(1, CHANS)
        )
        mine, passed = second_conv(place, laid, second_ring(two))
        total = mine + swapped(passed) + bias_2 + features.astype(F32)
        return total.astype(BF)

    volume = P("t", "h", ("z", "c"), None)
    weights = P(None, ("h", "z", "c"), None)
    return jax.shard_map(
        on_device,
        mesh=split,
        in_specs=(volume, P(), weights, P(), P(), weights, P()),
        out_specs=volume,
        check_vma=False,
    )
```

```python
import jax
import jax.numpy as jnp
from jax import lax
from jax.experimental import pallas as pl
from jax.experimental.pallas import tpu as pltpu
from jax.sharding import Mesh, PartitionSpec as P

AXES = ("t", "h", "z", "c")
SHIFT = ((0, 1, -1, 2), (0, -1, 1, 2))
MAIN = tuple(t for t in range(27) if t % 3 != 1)
PAIRED = (1, 4, 7, 10, 13, 16)
ALONE = (19, 22, 25)
GROUPS = len(MAIN) + len(ALONE)
CHANS = 384
LANES = 256
BF = jnp.bfloat16
F32 = jnp.float32
VMEM = pltpu.CompilerParams(vmem_limit_bytes=32 * 2**20)
whole = pl.BlockSpec(memory_space=pltpu.VMEM)


def move(x, sizes, source):
    def place(at):
        index = 0
        for coordinate, size in zip(at, sizes):
            index = index * size + coordinate % size
        return index

    pairs = []
    for index in range(sizes[0] * sizes[1] * sizes[2] * sizes[3]):
        rest, c = divmod(index, sizes[3])
        rest, z = divmod(rest, sizes[2])
        t, h = divmod(rest, sizes[1])
        at = source(t, h, z, c)
        if at is not None:
            pairs.append((place(at), index))
    return lax.ppermute(x, AXES, pairs)


def take(rows_ref, start, count, stride):
    return jnp.concatenate(
        [rows_ref[part, pl.ds(start, count, stride=stride)] for part in range(3)], axis=1
    )


def fold_kernel(k1_ref, k2_ref, out_ref, rows_ref):
    for which, k_ref in enumerate((k1_ref, k2_ref)):
        for r in range(6):
            for part in range(3):
                values = k_ref[r, :, 128 * part : 128 * part + 128]
                rows_ref[part, 32 * r : 32 * r + 27] = values.astype(F32)
        for g in range(GROUPS):
            if g < len(MAIN):
                low = take(rows_ref, MAIN[g], 6, 32)
                high = take(rows_ref, 64 * (g % 3) + PAIRED[g // 3], 2, 32)
            else:
                low = take(rows_ref, ALONE[g - len(MAIN)], 6, 32)
                high = jnp.zeros((2, CHANS), F32)
            out_ref[which, g] = jnp.concatenate([low, high], axis=0).astype(BF)


def fold(kernel_1, kernel_2):
    return pl.pallas_call(
        fold_kernel,
        out_shape=jax.ShapeDtypeStruct((2, GROUPS, 8, CHANS), BF),
        in_specs=[whole] * 2,
        out_specs=whole,
        scratch_shapes=[pltpu.VMEM((3, 192, 128), F32)],
        compiler_params=VMEM,
        name="fold",
    )(jnp.transpose(kernel_1, (1, 0, 2)), jnp.transpose(kernel_2, (1, 0, 2)))


def spread(spread_ref):
    t, h, z, c = (lax.axis_index(a) for a in AXES)
    lane = lax.broadcasted_iota(jnp.int32, (1, LANES), 1)
    j = lane & 7
    p = lane >> 3
    outer, inner, far = p >> 3, (p >> 1) & 3, p & 1
    t_of = (t + jnp.where(c == 0, inner, outer)) & 3
    h_of = (h + jnp.where(c == 0, outer, inner)) & 3
    sides = jnp.where((t_of == 1) == (c == 0), 1, 7)
    shift = jnp.where(t_of == 0, 0, jnp.where(t_of == 3, 2, sides))
    z_of = (z + shift + 4 * far) & 7
    base = 96 * h_of + 12 * z_of + 6 * c
    chan = lax.broadcasted_iota(jnp.int32, (CHANS, LANES), 0)
    spread_ref[0] = jnp.where(chan == jnp.where(j < 6, base + j, -1), 1.0, 0.0).astype(BF)
    for k in range(3):
        wanted = jnp.where(j >= 6, base + 2 * k + j - 6, -1)
        spread_ref[k + 1] = jnp.where(chan == wanted, 1.0, 0.0).astype(BF)


def activated(values, gain):
    square_mean = jnp.mean(values * values, axis=-1, keepdims=True)
    normed = values * lax.rsqrt(square_mean + 1e-06) * gain
    return normed * jax.nn.sigmoid(normed)


def lay_out(active, spread_ref, out_ref):
    count = active.shape[0]

    def put(slot, value, matrix):
        laid = jnp.dot(value, spread_ref[matrix], preferred_element_type=F32)
        out_ref[slot, 0] = laid.astype(BF)

    put(0, active.astype(BF), 0)
    one = pltpu.roll(active, count - 1, 0).astype(BF)
    put(1, one, 0)
    for k in range(3):
        put(3 + k, one, 1 + k)
    put(2, pltpu.roll(active, count - 2, 0).astype(BF), 0)


def first_layout_kernel(x_ref, gain_ref, out_ref, spread_ref):
    @pl.when(pl.program_id(0) == 0)
    def _():
        spread(spread_ref)

    values = x_ref[0].astype(F32).reshape(12 * 24, CHANS)
    lay_out(activated(values, gain_ref[...]), spread_ref, out_ref)


def first_layout(features, gain):
    return pl.pallas_call(
        first_layout_kernel,
        grid=(8,),
        out_shape=jax.ShapeDtypeStruct((6, 8, 12 * 24, LANES), BF),
        in_specs=[
            pl.BlockSpec((1, 12, 24, CHANS), lambda f: (f, 0, 0, 0)),
            pl.BlockSpec((1, CHANS), lambda f: (0, 0)),
        ],
        out_specs=pl.BlockSpec((6, 1, 12 * 24, LANES), lambda f: (0, f, 0, 0)),
        scratch_shapes=[pltpu.VMEM((4, CHANS, LANES), BF)],
        compiler_params=VMEM,
        name="first_layout",
    )(features, gain)


def second_layout_kernel(mine_ref, other_ref, bias_ref, gain_ref, out_ref, spread_ref):
    @pl.when(pl.program_id(0) == 0)
    def _():
        spread(spread_ref)

    t, h, z = (lax.axis_index(a) for a in AXES[:3])
    frame = pl.program_id(0) - 2 + 4 * t
    total = mine_ref[0] + other_ref[0].astype(F32) + bias_ref[...]
    active = activated(total.astype(BF).astype(F32), gain_ref[...])
    row = lax.broadcasted_iota(jnp.int32, (10, 24, 1), 0) + 8 * h - 1
    col = lax.broadcasted_iota(jnp.int32, (10, 24, 1), 1) + 20 * z - 1
    inside = (row >= 0) & (row < 32) & (col >= 0) & (col < 160) & (frame >= 0)
    active = active.reshape(10, 24, CHANS) * jnp.where(inside, 1.0, 0.0)
    lay_out(active.reshape(10 * 24, CHANS), spread_ref, out_ref)


def second_layout(mine, other, bias, gain):
    return pl.pallas_call(
        second_layout_kernel,
        grid=(6,),
        out_shape=jax.ShapeDtypeStruct((6, 6, 10 * 24, LANES), BF),
        in_specs=[
            pl.BlockSpec((1, 10 * 24, CHANS), lambda f: (f, 0, 0)),
            pl.BlockSpec((1, 10 * 24, CHANS), lambda f: (f, 0, 0)),
            pl.BlockSpec((1, CHANS), lambda f: (0, 0)),
            pl.BlockSpec((1, CHANS), lambda f: (0, 0)),
        ],
        out_specs=pl.BlockSpec((6, 1, 10 * 24, LANES), lambda f: (0, f, 0, 0)),
        scratch_shapes=[pltpu.VMEM((4, CHANS, LANES), BF)],
        compiler_params=VMEM,
        name="second_layout",
    )(mine, other, bias, gain)


def tap_sum(laid_ref, blocks, first, frames, count):
    def window(slot, tap):
        dt, start = tap // 9, 24 * (tap % 9 // 3)
        return jnp.concatenate(
            [laid_ref[slot, first + dt + i, start : start + count] for i in range(frames)], axis=0
        )

    total = None
    for g in range(GROUPS):
        if g < len(MAIN):
            left = window(MAIN[g] % 3, MAIN[g]) + window(3 + g % 3, PAIRED[g // 3])
        else:
            left = window(1, ALONE[g - len(MAIN)])
        right = jnp.concatenate([b[i, g] for b in blocks for i in range(b.shape[0])], axis=0)
        term = jnp.dot(left, right, preferred_element_type=F32)
        total = term if total is None else total + term
    return total


def first_conv_kernel(laid_ref, *refs):
    *blocks, mine_ref, sent_ref = refs
    total = tap_sum(laid_ref, blocks, 2 * pl.program_id(0), 2, 10 * 24)
    total = total.reshape(2, 10 * 24, CHANS)
    mine_ref[...] = total
    sent_ref[...] = total.astype(BF)


def first_conv(laid, blocks):
    out = pl.BlockSpec((2, 10 * 24, CHANS), lambda f: (f, 0, 0))
    return pl.pallas_call(
        first_conv_kernel,
        grid=(3,),
        out_shape=(
            jax.ShapeDtypeStruct((6, 10 * 24, CHANS), F32),
            jax.ShapeDtypeStruct((6, 10 * 24, CHANS), BF),
        ),
        in_specs=[whole] * (1 + len(blocks)),
        out_specs=(out, out),
        compiler_params=VMEM,
        name="first_conv",
    )(laid, *blocks)


def second_conv_kernel(laid_ref, *refs):
    *blocks, mine_ref, sent_ref, total_ref = refs
    total = tap_sum(laid_ref, blocks, 2 * pl.program_id(0), 2, 8 * 24)
    for part in range(3):
        total_ref[part] = total[:, 128 * part : 128 * part + 128]
    own = 10 * lax.axis_index("c")
    for f in range(2):
        for w in range(10):
            at = 192 * f + w
            mine_ref[f, w] = take(total_ref, at + own, 8, 24)
            sent_ref[f, w] = take(total_ref, at + 10 - own, 8, 24)


def second_conv(laid, blocks):
    out = pl.BlockSpec((2, 10, 8, CHANS), lambda f: (f, 0, 0, 0))
    return pl.pallas_call(
        second_conv_kernel,
        grid=(2,),
        out_shape=(
            jax.ShapeDtypeStruct((4, 10, 8, CHANS), F32),
            jax.ShapeDtypeStruct((4, 10, 8, CHANS), F32),
        ),
        in_specs=[whole] * (1 + len(blocks)),
        out_specs=(out, out),
        scratch_shapes=[pltpu.VMEM((3, 2 * 192, 128), F32)],
        compiler_params=VMEM,
        name="second_conv",
    )(laid, *blocks)


def solution(mesh):
    sizes = (mesh.shape["tm"], mesh.shape["height"], mesh.shape["width"] // 2, 2)
    split = Mesh(mesh.devices.reshape(sizes), AXES)

    def sent(x, source):
        return move(x, sizes, source)

    def along(first, step):
        def source(t, h, z, c):
            return (t + step, h, z, c) if (c == 0) == first else (t, h + step, z, c)

        return source

    def z_near(x):
        return sent(x, lambda t, h, z, c: (t, h, z + SHIFT[c][t], c))

    def z_far(x):
        return sent(x, lambda t, h, z, c: (t, h, z + SHIFT[c][t] + 4, c))

    def first_ring(x):
        up, down = sent(x, along(True, 1)), sent(x, along(True, -1))
        far = sent(x, along(True, 2))
        return [jnp.stack([x[i], up[i], far[i], down[i]]) for i in range(2)]

    def second_ring(x):
        return sent(x, along(False, 1)), sent(x, along(False, -1))

    def passed_on(up, down):
        return sent(up[:2], along(False, 1)), sent(down[2:], along(False, -1))

    def swapped(x):
        return sent(x, lambda t, h, z, c: (t, h, z, 1 - c))

    def inner(at, d):
        return at if all(0 <= a < s for a, s in zip(at, sizes)) else None

    def taller(x):
        earlier = sent(x, lambda t, h, z, c: inner((t - 1, h, z, c), 0))
        return jnp.concatenate([earlier, x], axis=0)

    def higher(x):
        above = sent(x[:, -2:], lambda t, h, z, c: inner((t, h - 1, z, c), 0))
        below = sent(x[:, :2], lambda t, h, z, c: inner((t, h + 1, z, c), 0))
        return jnp.concatenate([above, x, below], axis=1)

    def wider(x, core):
        edge = jnp.where(core == 0, x[:, :, :2], x[:, :, -2:])
        beside = sent(edge, lambda t, h, z, c: inner((t, h, z + 2 * c - 1, 1 - c), 0))
        return jnp.where(
            core == 0,
            jnp.concatenate([beside, x], axis=2),
            jnp.concatenate([x, beside], axis=2),
        )

    def joined(mine, core):
        other = swapped(mine)
        return jnp.where(
            core == 0,
            jnp.concatenate([mine, other], axis=2),
            jnp.concatenate([other, mine], axis=2),
        )

    def at_once(*values):
        return lax.optimization_barrier(values)

    def on_device(features, gain_1, kernel_1, bias_1, gain_2, kernel_2, bias_2):
        core = lax.axis_index("c")
        gains = [v.reshape(1, CHANS) for v in (gain_1, gain_2, bias_1)]
        both = fold(kernel_1, kernel_2)
        both = jnp.concatenate([z_near(both), z_far(both)], axis=2)
        both, wide = at_once(both, taller(features))
        one, two, wide = at_once(*first_ring(both), higher(wide))
        up, down = second_ring(one)
        up, down, wide, two = at_once(up, down, wider(wide, core), two)
        far = passed_on(up, down)
        next_up, next_down = second_ring(two)
        laid = first_layout(joined(wide, core), gains[0])
        mine, passed = first_conv(laid, (one, up, *far, down))
        next_up, next_down, passed = at_once(next_up, next_down, passed)
        far = passed_on(next_up, next_down)
        laid = second_layout(mine, swapped(passed), gains[2], gains[1])
        mine, passed = second_conv(laid, (two, next_up, *far, next_down))
        own = jnp.transpose(features, (0, 2, 1, 3)).astype(F32)
        total = mine + swapped(passed) + bias_2 + own
        return jnp.transpose(total.astype(BF), (0, 2, 1, 3))

    volume = P("t", "h", ("z", "c"), None)
    weights = P(None, ("h", "z", "c"), None)
    return jax.shard_map(
        on_device,
        mesh=split,
        in_specs=(volume, P(), weights, P(), P(), weights, P()),
        out_specs=volume,
        check_vma=False,
    )
```

```python
import functools

import jax
import jax.numpy as jnp
from jax import lax
from jax.experimental import pallas as pl
from jax.experimental.pallas import tpu as pltpu
from jax.sharding import Mesh, PartitionSpec as P

AXES = ("t", "h", "z", "c")
SHIFT = ((0, 1, -1, 2), (0, -1, 1, 2))
MAIN = tuple(t for t in range(27) if t % 3 != 1)
PAIRED = (1, 4, 7, 10, 13, 16)
ALONE = (19, 22, 25)
GROUPS = len(MAIN) + len(ALONE)
CHANS = 384
LANES = 256
BF = jnp.bfloat16
F32 = jnp.float32
VMEM = pltpu.CompilerParams(vmem_limit_bytes=32 * 2**20)
whole = pl.BlockSpec(memory_space=pltpu.VMEM)


def move(x, sizes, source):
    def place(at):
        index = 0
        for coordinate, size in zip(at, sizes):
            index = index * size + coordinate % size
        return index

    pairs = []
    for index in range(sizes[0] * sizes[1] * sizes[2] * sizes[3]):
        rest, c = divmod(index, sizes[3])
        rest, z = divmod(rest, sizes[2])
        t, h = divmod(rest, sizes[1])
        at = source(t, h, z, c)
        if at is not None:
            pairs.append((place(at), index))
    return lax.ppermute(x, AXES, pairs)


def take(rows_ref, start, count, stride):
    return jnp.concatenate(
        [rows_ref[part, pl.ds(start, count, stride=stride)] for part in range(3)], axis=1
    )


def fold_kernel(k1_ref, k2_ref, out_ref, rows_ref):
    for which, k_ref in enumerate((k1_ref, k2_ref)):
        for r in range(6):
            for part in range(3):
                values = k_ref[r, :, 128 * part : 128 * part + 128]
                rows_ref[part, 32 * r : 32 * r + 27] = values.astype(F32)
        for g in range(GROUPS):
            if g < len(MAIN):
                low = take(rows_ref, MAIN[g], 6, 32)
                high = take(rows_ref, 64 * (g % 3) + PAIRED[g // 3], 2, 32)
            else:
                low = take(rows_ref, ALONE[g - len(MAIN)], 6, 32)
                high = jnp.zeros((2, CHANS), F32)
            out_ref[which, g] = jnp.concatenate([low, high], axis=0).astype(BF)


def fold(kernel_1, kernel_2):
    return pl.pallas_call(
        fold_kernel,
        out_shape=jax.ShapeDtypeStruct((2, GROUPS, 8, CHANS), BF),
        in_specs=[whole] * 2,
        out_specs=whole,
        scratch_shapes=[pltpu.VMEM((3, 192, 128), F32)],
        compiler_params=VMEM,
        name="fold",
    )(jnp.transpose(kernel_1, (1, 0, 2)), jnp.transpose(kernel_2, (1, 0, 2)))


def spread(spread_ref):
    t, h, z, c = (lax.axis_index(a) for a in AXES)
    lane = lax.broadcasted_iota(jnp.int32, (1, LANES), 1)
    j = lane & 7
    p = lane >> 3
    outer, inner, far = p >> 3, (p >> 1) & 3, p & 1
    t_of = (t + jnp.where(c == 0, inner, outer)) & 3
    h_of = (h + jnp.where(c == 0, outer, inner)) & 3
    sides = jnp.where((t_of == 1) == (c == 0), 1, 7)
    shift = jnp.where(t_of == 0, 0, jnp.where(t_of == 3, 2, sides))
    z_of = (z + shift + 4 * far) & 7
    base = 96 * h_of + 12 * z_of + 6 * c
    chan = lax.broadcasted_iota(jnp.int32, (CHANS, LANES), 0)
    spread_ref[0] = jnp.where(chan == jnp.where(j < 6, base + j, -1), 1.0, 0.0).astype(BF)
    for k in range(3):
        wanted = jnp.where(j >= 6, base + 2 * k + j - 6, -1)
        spread_ref[k + 1] = jnp.where(chan == wanted, 1.0, 0.0).astype(BF)


def activated(values, gain):
    square_mean = jnp.mean(values * values, axis=-1, keepdims=True)
    normed = values * lax.rsqrt(square_mean + 1e-06) * gain
    return normed * jax.nn.sigmoid(normed)


def lay_out(active, spread_ref, out_ref):
    count = active.shape[0]

    def put(slot, value, matrix):
        laid = jnp.dot(value, spread_ref[matrix], preferred_element_type=F32)
        out_ref[slot, 0] = laid.astype(BF)

    put(0, active.astype(BF), 0)
    one = pltpu.roll(active, count - 1, 0).astype(BF)
    put(1, one, 0)
    for k in range(3):
        put(3 + k, one, 1 + k)
    put(2, pltpu.roll(active, count - 2, 0).astype(BF), 0)


def first_layout_kernel(x_ref, gain_ref, out_ref, spread_ref):
    @pl.when(pl.program_id(0) == 0)
    def _():
        spread(spread_ref)

    values = x_ref[0].astype(F32).reshape(12 * 24, CHANS)
    lay_out(activated(values, gain_ref[...]), spread_ref, out_ref)


def first_layout(features, gain):
    return pl.pallas_call(
        first_layout_kernel,
        grid=(8,),
        out_shape=jax.ShapeDtypeStruct((6, 8, 12 * 24, LANES), BF),
        in_specs=[
            pl.BlockSpec((1, 12, 24, CHANS), lambda f: (f, 0, 0, 0)),
            pl.BlockSpec((1, CHANS), lambda f: (0, 0)),
        ],
        out_specs=pl.BlockSpec((6, 1, 12 * 24, LANES), lambda f: (0, f, 0, 0)),
        scratch_shapes=[pltpu.VMEM((4, CHANS, LANES), BF)],
        compiler_params=VMEM,
        name="first_layout",
    )(features, gain)


def second_layout_kernel(mine_ref, other_ref, bias_ref, gain_ref, out_ref, spread_ref):
    @pl.when(pl.program_id(0) == 0)
    def _():
        spread(spread_ref)

    t, h, z = (lax.axis_index(a) for a in AXES[:3])
    frame = pl.program_id(0) - 2 + 4 * t
    total = mine_ref[0] + other_ref[0].astype(F32) + bias_ref[...]
    active = activated(total.astype(BF).astype(F32), gain_ref[...])
    row = lax.broadcasted_iota(jnp.int32, (10, 24, 1), 0) + 8 * h - 1
    col = lax.broadcasted_iota(jnp.int32, (10, 24, 1), 1) + 20 * z - 1
    inside = (row >= 0) & (row < 32) & (col >= 0) & (col < 160) & (frame >= 0)
    active = active.reshape(10, 24, CHANS) * jnp.where(inside, 1.0, 0.0)
    lay_out(active.reshape(10 * 24, CHANS), spread_ref, out_ref)


def second_layout(mine, other, bias, gain):
    return pl.pallas_call(
        second_layout_kernel,
        grid=(6,),
        out_shape=jax.ShapeDtypeStruct((6, 6, 10 * 24, LANES), BF),
        in_specs=[
            pl.BlockSpec((1, 10 * 24, CHANS), lambda f: (f, 0, 0)),
            pl.BlockSpec((1, 10 * 24, CHANS), lambda f: (f, 0, 0)),
            pl.BlockSpec((1, CHANS), lambda f: (0, 0)),
            pl.BlockSpec((1, CHANS), lambda f: (0, 0)),
        ],
        out_specs=pl.BlockSpec((6, 1, 10 * 24, LANES), lambda f: (0, f, 0, 0)),
        scratch_shapes=[pltpu.VMEM((4, CHANS, LANES), BF)],
        compiler_params=VMEM,
        name="second_layout",
    )(mine, other, bias, gain)


def left_of(laid_ref, g, first, frames, count, lanes):
    def window(slot, tap):
        dt, start = tap // 9, 24 * (tap % 9 // 3)
        at = slice(start, start + count)
        return jnp.concatenate(
            [laid_ref[slot, first + dt + i, at, lanes] for i in range(frames)], axis=0
        )

    if g < len(MAIN):
        return window(MAIN[g] % 3, MAIN[g]) + window(3 + g % 3, PAIRED[g // 3])
    return window(1, ALONE[g - len(MAIN)])


def near_sum(laid_ref, blocks, first, frames, count):
    zeros = jnp.zeros((LANES // 4, CHANS), BF)
    total = None
    for g in range(GROUPS):
        rows = [b[i, g] for b in blocks for i in range(2)]
        right = jnp.concatenate(rows[:8] + [zeros] + rows[8:], axis=0)
        left = left_of(laid_ref, g, first, frames, count, slice(0, LANES))
        term = jnp.dot(left, right, preferred_element_type=F32)
        total = term if total is None else total + term
    return total


def far_sum(laid_ref, blocks, first, frames, count):
    total = None
    for base in range(0, GROUPS, 4):
        groups = range(base, min(base + 4, GROUPS))
        left, right = [], []
        for g in groups:
            left.append(left_of(laid_ref, g, first, frames, count, slice(128, 256))[:, :64])
            right += [b[i, g] for b in blocks for i in range(2)]
        left, right = jnp.concatenate(left, axis=1), jnp.concatenate(right, axis=0)
        term = jnp.dot(left, right, preferred_element_type=F32)
        total = term if total is None else total + term
    return total


def near_kernel(frames, count, laid_ref, *refs):
    *blocks, out_ref = refs
    total = near_sum(laid_ref, blocks, 2 * pl.program_id(0), 2, count)
    out_ref[...] = total.reshape(2, count, CHANS)


def near_conv(laid, blocks, frames, count):
    return pl.pallas_call(
        functools.partial(near_kernel, frames, count),
        grid=(frames // 2,),
        out_shape=jax.ShapeDtypeStruct((frames, count, CHANS), F32),
        in_specs=[whole] * (1 + len(blocks)),
        out_specs=pl.BlockSpec((2, count, CHANS), lambda f: (f, 0, 0)),
        compiler_params=VMEM,
        name="near_conv",
    )(laid, *blocks)


def first_conv_kernel(laid_ref, b0, b1, near_ref, mine_ref, sent_ref):
    total = far_sum(laid_ref, (b0, b1), 2 * pl.program_id(0), 2, 10 * 24)
    total = near_ref[...] + total.reshape(2, 10 * 24, CHANS)
    mine_ref[...] = total
    sent_ref[...] = total.astype(BF)


def first_conv(laid, blocks, near):
    out = pl.BlockSpec((2, 10 * 24, CHANS), lambda f: (f, 0, 0))
    return pl.pallas_call(
        first_conv_kernel,
        grid=(3,),
        out_shape=(
            jax.ShapeDtypeStruct((6, 10 * 24, CHANS), F32),
            jax.ShapeDtypeStruct((6, 10 * 24, CHANS), BF),
        ),
        in_specs=[whole] * 3 + [out],
        out_specs=(out, out),
        compiler_params=VMEM,
        name="first_conv",
    )(laid, *blocks, near)


def second_conv_kernel(laid_ref, b0, b1, near_ref, mine_ref, sent_ref, total_ref):
    total = far_sum(laid_ref, (b0, b1), 2 * pl.program_id(0), 2, 8 * 24)
    total = near_ref[...].reshape(2 * 192, CHANS) + total
    for part in range(3):
        total_ref[part] = total[:, 128 * part : 128 * part + 128]
    own = 10 * lax.axis_index("c")
    for f in range(2):
        for w in range(10):
            at = 192 * f + w
            mine_ref[f, w] = take(total_ref, at + own, 8, 24)
            sent_ref[f, w] = take(total_ref, at + 10 - own, 8, 24)


def second_conv(laid, blocks, near):
    out = pl.BlockSpec((2, 10, 8, CHANS), lambda f: (f, 0, 0, 0))
    return pl.pallas_call(
        second_conv_kernel,
        grid=(2,),
        out_shape=(
            jax.ShapeDtypeStruct((4, 10, 8, CHANS), F32),
            jax.ShapeDtypeStruct((4, 10, 8, CHANS), F32),
        ),
        in_specs=[whole] * 3 + [pl.BlockSpec((2, 8 * 24, CHANS), lambda f: (f, 0, 0))],
        out_specs=(out, out),
        scratch_shapes=[pltpu.VMEM((3, 2 * 192, 128), F32)],
        compiler_params=VMEM,
        name="second_conv",
    )(laid, *blocks, near)


def solution(mesh):
    sizes = (mesh.shape["tm"], mesh.shape["height"], mesh.shape["width"] // 2, 2)
    split = Mesh(mesh.devices.reshape(sizes), AXES)

    def sent(x, source):
        return move(x, sizes, source)

    def along(first, step):
        def source(t, h, z, c):
            return (t + step, h, z, c) if (c == 0) == first else (t, h + step, z, c)

        return source

    def z_near(x):
        return sent(x, lambda t, h, z, c: (t, h, z + SHIFT[c][t], c))

    def z_far(x):
        return sent(x, lambda t, h, z, c: (t, h, z + SHIFT[c][t] + 4, c))

    def first_ring(x):
        up, down = sent(x, along(True, 1)), sent(x, along(True, -1))
        far = sent(x, along(True, 2))
        return [(jnp.stack([x[i], up[i]]), jnp.stack([far[i], down[i]])) for i in range(2)]

    def second_ring(x):
        return sent(x[0], along(False, 1)), sent(x[1], along(False, -1))

    def second_ring_rest(x):
        return sent(x[1], along(False, 1)), sent(x[0], along(False, -1))

    def passed_on(first_up, last_down):
        return sent(first_up, along(False, 1)), sent(last_down, along(False, -1))

    def in_order(x, first_up, last_down, last_up, first_down):
        return (*x, first_up, last_up, first_down, last_down)

    def swapped(x):
        return sent(x, lambda t, h, z, c: (t, h, z, 1 - c))

    def inner(at, d):
        return at if all(0 <= a < s for a, s in zip(at, sizes)) else None

    def taller(x):
        earlier = sent(x, lambda t, h, z, c: inner((t - 1, h, z, c), 0))
        return jnp.concatenate([earlier, x], axis=0)

    def higher(x):
        above = sent(x[:, -2:], lambda t, h, z, c: inner((t, h - 1, z, c), 0))
        below = sent(x[:, :2], lambda t, h, z, c: inner((t, h + 1, z, c), 0))
        return jnp.concatenate([above, x, below], axis=1)

    def wider(x, core):
        edge = jnp.where(core == 0, x[:, :, :2], x[:, :, -2:])
        beside = sent(edge, lambda t, h, z, c: inner((t, h, z + 2 * c - 1, 1 - c), 0))
        return jnp.where(
            core == 0,
            jnp.concatenate([beside, x], axis=2),
            jnp.concatenate([x, beside], axis=2),
        )

    def joined(mine, core):
        other = swapped(mine)
        return jnp.where(
            core == 0,
            jnp.concatenate([mine, other], axis=2),
            jnp.concatenate([other, mine], axis=2),
        )

    def at_once(*values):
        return lax.optimization_barrier(values)

    def on_device(features, gain_1, kernel_1, bias_1, gain_2, kernel_2, bias_2):
        core = lax.axis_index("c")
        gains = [v.reshape(1, CHANS) for v in (gain_1, gain_2, bias_1)]
        both = fold(kernel_1, kernel_2)
        both = jnp.concatenate([z_near(both), z_far(both)], axis=2)
        both, wide = at_once(both, higher(taller(features)))
        one, two = first_ring(both)
        (one, two), wide = at_once((one, two), wider(wide, core))
        ends, rest = second_ring(one), second_ring_rest(one)
        laid = first_layout(joined(wide, core), gains[0])
        ends, laid, two = at_once(ends, laid, two)
        far = passed_on(*ends)
        rest = at_once(*rest)
        next_ends = second_ring(two)
        near = near_conv(laid, in_order(one, *ends, *rest), 6, 10 * 24)
        far, near, next_ends = at_once(far, near, next_ends)
        mine, passed = first_conv(laid, far, near)
        next_rest = second_ring_rest(two)
        far = passed_on(*next_ends)
        laid = second_layout(mine, swapped(passed), gains[2], gains[1])
        near = near_conv(laid, in_order(two, *next_ends, *next_rest), 4, 8 * 24)
        mine, passed = second_conv(laid, far, near)
        own = jnp.transpose(features, (0, 2, 1, 3)).astype(F32)
        total = mine + swapped(passed) + bias_2 + own
        return jnp.transpose(total.astype(BF), (0, 2, 1, 3))

    volume = P("t", "h", ("z", "c"), None)
    weights = P(None, ("h", "z", "c"), None)
    return jax.shard_map(
        on_device,
        mesh=split,
        in_specs=(volume, P(), weights, P(), P(), weights, P()),
        out_specs=volume,
        check_vma=False,
    )
```

```python
import functools

import jax
import jax.numpy as jnp
from jax import lax
from jax.experimental import pallas as pl
from jax.experimental.pallas import tpu as pltpu
from jax.sharding import Mesh, PartitionSpec as P

AXES = ("t", "h", "z", "c")
SHIFT = ((0, 1, -1, 2), (0, -1, 1, 2))
MAIN = tuple(t for t in range(27) if t % 3 != 1)
PAIRED = (1, 4, 7, 10, 13, 16)
ALONE = (19, 22, 25)
GROUPS = len(MAIN) + len(ALONE)
CHANS = 384
LANES = 256
BF = jnp.bfloat16
F32 = jnp.float32
VMEM = pltpu.CompilerParams(vmem_limit_bytes=32 * 2**20)
whole = pl.BlockSpec(memory_space=pltpu.VMEM)


def move(x, sizes, source):
    def place(at):
        index = 0
        for coordinate, size in zip(at, sizes):
            index = index * size + coordinate % size
        return index

    pairs = []
    for index in range(sizes[0] * sizes[1] * sizes[2] * sizes[3]):
        rest, c = divmod(index, sizes[3])
        rest, z = divmod(rest, sizes[2])
        t, h = divmod(rest, sizes[1])
        at = source(t, h, z, c)
        if at is not None:
            pairs.append((place(at), index))
    return lax.ppermute(x, AXES, pairs)


def take(rows_ref, start, count, stride):
    return jnp.concatenate(
        [rows_ref[part, pl.ds(start, count, stride=stride)] for part in range(3)], axis=1
    )


def fold_kernel(k1_ref, k2_ref, out_ref, rows_ref):
    for which, k_ref in enumerate((k1_ref, k2_ref)):
        for r in range(6):
            for part in range(3):
                values = k_ref[r, :, 128 * part : 128 * part + 128]
                rows_ref[part, 32 * r : 32 * r + 27] = values.astype(F32)
        for g in range(GROUPS):
            if g < len(MAIN):
                low = take(rows_ref, MAIN[g], 6, 32)
                high = take(rows_ref, 64 * (g % 3) + PAIRED[g // 3], 2, 32)
            else:
                low = take(rows_ref, ALONE[g - len(MAIN)], 6, 32)
                high = jnp.zeros((2, CHANS), F32)
            out_ref[which, g] = jnp.concatenate([low, high], axis=0).astype(BF)


def fold(kernel_1, kernel_2):
    return pl.pallas_call(
        fold_kernel,
        out_shape=jax.ShapeDtypeStruct((2, GROUPS, 8, CHANS), BF),
        in_specs=[whole] * 2,
        out_specs=whole,
        scratch_shapes=[pltpu.VMEM((3, 192, 128), F32)],
        compiler_params=VMEM,
        name="fold",
    )(jnp.transpose(kernel_1, (1, 0, 2)), jnp.transpose(kernel_2, (1, 0, 2)))


def spread(spread_ref):
    t, h, z, c = (lax.axis_index(a) for a in AXES)
    lane = lax.broadcasted_iota(jnp.int32, (1, LANES), 1)
    j = lane & 7
    p = lane >> 3
    outer, inner, far = p >> 3, (p >> 1) & 3, p & 1
    t_of = (t + jnp.where(c == 0, inner, outer)) & 3
    h_of = (h + jnp.where(c == 0, outer, inner)) & 3
    sides = jnp.where((t_of == 1) == (c == 0), 1, 7)
    shift = jnp.where(t_of == 0, 0, jnp.where(t_of == 3, 2, sides))
    z_of = (z + shift + 4 * far) & 7
    base = 96 * h_of + 12 * z_of + 6 * c
    chan = lax.broadcasted_iota(jnp.int32, (CHANS, LANES), 0)
    spread_ref[...] = jnp.where(chan == jnp.where(j < 6, base + j, -1), 1.0, 0.0).astype(BF)


def activated(values, gain):
    square_mean = jnp.mean(values * values, axis=-1, keepdims=True)
    normed = values * lax.rsqrt(square_mean + 1e-06) * gain
    return normed * jax.nn.sigmoid(normed)


def lay_out(active, spread_ref, out_ref):
    count = active.shape[0]
    laid = jnp.dot(active.astype(BF), spread_ref[...], preferred_element_type=F32)
    one = pltpu.roll(laid, count - 1, 0)
    out_ref[0, 0] = laid.astype(BF)
    out_ref[1, 0] = one.astype(BF)
    out_ref[2, 0] = pltpu.roll(laid, count - 2, 0).astype(BF)
    last = (lax.broadcasted_iota(jnp.int32, (count, 128), 1) & 7) >= 6
    for k in range(3):
        for part in (slice(0, 128), slice(128, 256)):
            pair = pltpu.roll(one[:, part], 6 - 2 * k, 1)
            out_ref[3 + k, 0, :, part] = jnp.where(last, pair, 0.0).astype(BF)


def first_layout_kernel(x_ref, gain_ref, out_ref, spread_ref):
    @pl.when(pl.program_id(0) == 0)
    def _():
        spread(spread_ref)

    values = x_ref[0].astype(F32).reshape(12 * 24, CHANS)
    lay_out(activated(values, gain_ref[...]), spread_ref, out_ref)


def first_layout(features, gain):
    return pl.pallas_call(
        first_layout_kernel,
        grid=(8,),
        out_shape=jax.ShapeDtypeStruct((6, 8, 12 * 24, LANES), BF),
        in_specs=[
            pl.BlockSpec((1, 12, 24, CHANS), lambda f: (f, 0, 0, 0)),
            pl.BlockSpec((1, CHANS), lambda f: (0, 0)),
        ],
        out_specs=pl.BlockSpec((6, 1, 12 * 24, LANES), lambda f: (0, f, 0, 0)),
        scratch_shapes=[pltpu.VMEM((CHANS, LANES), BF)],
        compiler_params=VMEM,
        name="first_layout",
    )(features, gain)


def second_layout_kernel(mine_ref, other_ref, bias_ref, gain_ref, out_ref, spread_ref):
    @pl.when(pl.program_id(0) == 0)
    def _():
        spread(spread_ref)

    t, h, z = (lax.axis_index(a) for a in AXES[:3])
    frame = pl.program_id(0) - 2 + 4 * t
    total = mine_ref[0] + other_ref[0].astype(F32) + bias_ref[...]
    active = activated(total.astype(BF).astype(F32), gain_ref[...])
    row = lax.broadcasted_iota(jnp.int32, (10, 24, 1), 0) + 8 * h - 1
    col = lax.broadcasted_iota(jnp.int32, (10, 24, 1), 1) + 20 * z - 1
    inside = (row >= 0) & (row < 32) & (col >= 0) & (col < 160) & (frame >= 0)
    active = active.reshape(10, 24, CHANS) * jnp.where(inside, 1.0, 0.0)
    lay_out(active.reshape(10 * 24, CHANS), spread_ref, out_ref)


def second_layout(mine, other, bias, gain):
    return pl.pallas_call(
        second_layout_kernel,
        grid=(6,),
        out_shape=jax.ShapeDtypeStruct((6, 6, 10 * 24, LANES), BF),
        in_specs=[
            pl.BlockSpec((1, 10 * 24, CHANS), lambda f: (f, 0, 0)),
            pl.BlockSpec((1, 10 * 24, CHANS), lambda f: (f, 0, 0)),
            pl.BlockSpec((1, CHANS), lambda f: (0, 0)),
            pl.BlockSpec((1, CHANS), lambda f: (0, 0)),
        ],
        out_specs=pl.BlockSpec((6, 1, 10 * 24, LANES), lambda f: (0, f, 0, 0)),
        scratch_shapes=[pltpu.VMEM((CHANS, LANES), BF)],
        compiler_params=VMEM,
        name="second_layout",
    )(mine, other, bias, gain)


def left_of(laid_ref, g, first, frames, count, lanes):
    def window(slot, tap):
        dt, start = tap // 9, 24 * (tap % 9 // 3)
        at = slice(start, start + count)
        return jnp.concatenate(
            [laid_ref[slot, first + dt + i, at, lanes] for i in range(frames)], axis=0
        )

    if g < len(MAIN):
        return window(MAIN[g] % 3, MAIN[g]) + window(3 + g % 3, PAIRED[g // 3])
    return window(1, ALONE[g - len(MAIN)])


def near_sum(laid_ref, blocks, first, frames, count):
    zeros = jnp.zeros((LANES // 4, CHANS), BF)
    total = None
    for g in range(GROUPS):
        rows = [b[i, g] for b in blocks for i in range(2)]
        right = jnp.concatenate(rows[:8] + [zeros] + rows[8:], axis=0)
        left = left_of(laid_ref, g, first, frames, count, slice(0, LANES))
        term = jnp.dot(left, right, preferred_element_type=F32)
        total = term if total is None else total + term
    return total


def far_sum(laid_ref, blocks, first, frames, count):
    total = None
    for base in range(0, GROUPS, 4):
        groups = range(base, min(base + 4, GROUPS))
        left, right = [], []
        for g in groups:
            left.append(left_of(laid_ref, g, first, frames, count, slice(128, 256))[:, :64])
            right += [b[i, g] for b in blocks for i in range(2)]
        left, right = jnp.concatenate(left, axis=1), jnp.concatenate(right, axis=0)
        term = jnp.dot(left, right, preferred_element_type=F32)
        total = term if total is None else total + term
    return total


def near_kernel(frames, count, laid_ref, *refs):
    *blocks, out_ref = refs
    total = near_sum(laid_ref, blocks, 2 * pl.program_id(0), 2, count)
    out_ref[...] = total.reshape(2, count, CHANS)


def near_conv(laid, blocks, frames, count):
    return pl.pallas_call(
        functools.partial(near_kernel, frames, count),
        grid=(frames // 2,),
        out_shape=jax.ShapeDtypeStruct((frames, count, CHANS), F32),
        in_specs=[whole] * (1 + len(blocks)),
        out_specs=pl.BlockSpec((2, count, CHANS), lambda f: (f, 0, 0)),
        compiler_params=VMEM,
        name="near_conv",
    )(laid, *blocks)


def first_conv_kernel(laid_ref, b0, b1, near_ref, mine_ref, sent_ref):
    total = far_sum(laid_ref, (b0, b1), 2 * pl.program_id(0), 2, 10 * 24)
    total = near_ref[...] + total.reshape(2, 10 * 24, CHANS)
    mine_ref[...] = total
    sent_ref[...] = total.astype(BF)


def first_conv(laid, blocks, near):
    out = pl.BlockSpec((2, 10 * 24, CHANS), lambda f: (f, 0, 0))
    return pl.pallas_call(
        first_conv_kernel,
        grid=(3,),
        out_shape=(
            jax.ShapeDtypeStruct((6, 10 * 24, CHANS), F32),
            jax.ShapeDtypeStruct((6, 10 * 24, CHANS), BF),
        ),
        in_specs=[whole] * 3 + [out],
        out_specs=(out, out),
        compiler_params=VMEM,
        name="first_conv",
    )(laid, *blocks, near)


def second_conv_kernel(laid_ref, b0, b1, near_ref, mine_ref, sent_ref, total_ref):
    total = far_sum(laid_ref, (b0, b1), 2 * pl.program_id(0), 2, 8 * 24)
    total = near_ref[...].reshape(2 * 192, CHANS) + total
    for part in range(3):
        total_ref[part] = total[:, 128 * part : 128 * part + 128]
    own = 10 * lax.axis_index("c")
    for f in range(2):
        for w in range(10):
            at = 192 * f + w
            mine_ref[f, w] = take(total_ref, at + own, 8, 24)
            sent_ref[f, w] = take(total_ref, at + 10 - own, 8, 24)


def second_conv(laid, blocks, near):
    out = pl.BlockSpec((2, 10, 8, CHANS), lambda f: (f, 0, 0, 0))
    return pl.pallas_call(
        second_conv_kernel,
        grid=(2,),
        out_shape=(
            jax.ShapeDtypeStruct((4, 10, 8, CHANS), F32),
            jax.ShapeDtypeStruct((4, 10, 8, CHANS), F32),
        ),
        in_specs=[whole] * 3 + [pl.BlockSpec((2, 8 * 24, CHANS), lambda f: (f, 0, 0))],
        out_specs=(out, out),
        scratch_shapes=[pltpu.VMEM((3, 2 * 192, 128), F32)],
        compiler_params=VMEM,
        name="second_conv",
    )(laid, *blocks, near)


def solution(mesh):
    sizes = (mesh.shape["tm"], mesh.shape["height"], mesh.shape["width"] // 2, 2)
    split = Mesh(mesh.devices.reshape(sizes), AXES)

    def sent(x, source):
        return move(x, sizes, source)

    def along(first, step):
        def source(t, h, z, c):
            return (t + step, h, z, c) if (c == 0) == first else (t, h + step, z, c)

        return source

    def z_near(x):
        return sent(x, lambda t, h, z, c: (t, h, z + SHIFT[c][t], c))

    def z_far(x):
        return sent(x, lambda t, h, z, c: (t, h, z + SHIFT[c][t] + 4, c))

    def first_ring(x):
        up, down = sent(x, along(True, 1)), sent(x, along(True, -1))
        far = sent(x, along(True, 2))
        return [(jnp.stack([x[i], up[i]]), jnp.stack([far[i], down[i]])) for i in range(2)]

    def second_ring(x):
        return sent(x[0], along(False, 1)), sent(x[1], along(False, -1))

    def second_ring_rest(x):
        return sent(x[1], along(False, 1)), sent(x[0], along(False, -1))

    def passed_on(first_up, last_down):
        return sent(first_up, along(False, 1)), sent(last_down, along(False, -1))

    def in_order(x, first_up, last_down, last_up, first_down):
        return (*x, first_up, last_up, first_down, last_down)

    def swapped(x):
        return sent(x, lambda t, h, z, c: (t, h, z, 1 - c))

    def inner(at, d):
        return at if all(0 <= a < s for a, s in zip(at, sizes)) else None

    def taller(x):
        earlier = sent(x, lambda t, h, z, c: inner((t - 1, h, z, c), 0))
        return jnp.concatenate([earlier, x], axis=0)

    def higher(x):
        above = sent(x[:, -2:], lambda t, h, z, c: inner((t, h - 1, z, c), 0))
        below = sent(x[:, :2], lambda t, h, z, c: inner((t, h + 1, z, c), 0))
        return jnp.concatenate([above, x, below], axis=1)

    def wider(x, core):
        edge = jnp.where(core == 0, x[:, :, :2], x[:, :, -2:])
        beside = sent(edge, lambda t, h, z, c: inner((t, h, z + 2 * c - 1, 1 - c), 0))
        return jnp.where(
            core == 0,
            jnp.concatenate([beside, x], axis=2),
            jnp.concatenate([x, beside], axis=2),
        )

    def joined(mine, core):
        other = swapped(mine)
        return jnp.where(
            core == 0,
            jnp.concatenate([mine, other], axis=2),
            jnp.concatenate([other, mine], axis=2),
        )

    def at_once(*values):
        return lax.optimization_barrier(values)

    def on_device(features, gain_1, kernel_1, bias_1, gain_2, kernel_2, bias_2):
        core = lax.axis_index("c")
        gains = [v.reshape(1, CHANS) for v in (gain_1, gain_2, bias_1)]
        both = fold(kernel_1, kernel_2)
        both = jnp.concatenate([z_near(both), z_far(both)], axis=2)
        both, wide = at_once(both, higher(taller(features)))
        one, two = first_ring(both)
        (one, two), wide = at_once((one, two), joined(wider(wide, core), core))
        ends, rest = second_ring(one), second_ring_rest(one)
        ends, laid, two = at_once(ends, first_layout(wide, gains[0]), two)
        far = passed_on(*ends)
        next_ends = second_ring(two)
        near = near_conv(laid, in_order(one, *ends, *at_once(*rest)), 6, 10 * 24)
        far, near, next_ends = at_once(far, near, next_ends)
        mine, passed = first_conv(laid, far, near)
        next_rest = second_ring_rest(two)
        far = passed_on(*next_ends)
        laid = second_layout(mine, swapped(passed), gains[2], gains[1])
        near = near_conv(laid, in_order(two, *next_ends, *next_rest), 4, 8 * 24)
        mine, passed = second_conv(laid, far, near)
        own = jnp.transpose(features, (0, 2, 1, 3)).astype(F32)
        total = mine + swapped(passed) + bias_2 + own
        return jnp.transpose(total.astype(BF), (0, 2, 1, 3))

    volume = P("t", "h", ("z", "c"), None)
    weights = P(None, ("h", "z", "c"), None)
    return jax.shard_map(
        on_device,
        mesh=split,
        in_specs=(volume, P(), weights, P(), P(), weights, P()),
        out_specs=volume,
        check_vma=False,
    )
```

```python
import functools

import jax
import jax.numpy as jnp
from jax import lax
from jax.experimental import pallas as pl
from jax.experimental.pallas import tpu as pltpu
from jax.sharding import Mesh, PartitionSpec as P

AXES = ("t", "h", "z", "c")
SHIFT = ((0, 1, -1, 2), (0, -1, 1, 2))
MAIN = tuple(t for t in range(27) if t % 3 != 1)
PAIRED = (1, 4, 7, 10, 13, 16)
ALONE = (19, 22, 25)
GROUPS = len(MAIN) + len(ALONE)
CHANS = 384
LANES = 256
BF = jnp.bfloat16
F32 = jnp.float32
VMEM = pltpu.CompilerParams(vmem_limit_bytes=32 * 2**20)
whole = pl.BlockSpec(memory_space=pltpu.VMEM)


def move(x, sizes, source):
    def place(at):
        index = 0
        for coordinate, size in zip(at, sizes):
            index = index * size + coordinate % size
        return index

    pairs = []
    for index in range(sizes[0] * sizes[1] * sizes[2] * sizes[3]):
        rest, c = divmod(index, sizes[3])
        rest, z = divmod(rest, sizes[2])
        t, h = divmod(rest, sizes[1])
        at = source(t, h, z, c)
        if at is not None:
            pairs.append((place(at), index))
    return lax.ppermute(x, AXES, pairs)


def take(rows_ref, start, count, stride):
    return jnp.concatenate(
        [rows_ref[part, pl.ds(start, count, stride=stride)] for part in range(3)], axis=1
    )


def fold_kernel(k1_ref, k2_ref, out_ref, rows_ref):
    for which, k_ref in enumerate((k1_ref, k2_ref)):
        for r in range(6):
            for part in range(3):
                values = k_ref[r, :, 128 * part : 128 * part + 128]
                rows_ref[part, 32 * r : 32 * r + 27] = values.astype(F32)
        for g in range(GROUPS):
            if g < len(MAIN):
                low = take(rows_ref, MAIN[g], 6, 32)
                high = take(rows_ref, 64 * (g % 3) + PAIRED[g // 3], 2, 32)
            else:
                low = take(rows_ref, ALONE[g - len(MAIN)], 6, 32)
                high = jnp.zeros((2, CHANS), F32)
            out_ref[which, g] = jnp.concatenate([low, high], axis=0).astype(BF)


def fold(kernel_1, kernel_2):
    return pl.pallas_call(
        fold_kernel,
        out_shape=jax.ShapeDtypeStruct((2, GROUPS, 8, CHANS), BF),
        in_specs=[whole] * 2,
        out_specs=whole,
        scratch_shapes=[pltpu.VMEM((3, 192, 128), F32)],
        compiler_params=VMEM,
        name="fold",
    )(jnp.transpose(kernel_1, (1, 0, 2)), jnp.transpose(kernel_2, (1, 0, 2)))


def spread(spread_ref):
    t, h, z, c = (lax.axis_index(a) for a in AXES)
    lane = lax.broadcasted_iota(jnp.int32, (1, LANES), 1)
    j = lane & 7
    p = lane >> 3
    outer, inner, far = p >> 3, (p >> 1) & 3, p & 1
    t_of = (t + jnp.where(c == 0, inner, outer)) & 3
    h_of = (h + jnp.where(c == 0, outer, inner)) & 3
    sides = jnp.where((t_of == 1) == (c == 0), 1, 7)
    shift = jnp.where(t_of == 0, 0, jnp.where(t_of == 3, 2, sides))
    z_of = (z + shift + 4 * far) & 7
    base = 96 * h_of + 12 * z_of + 6 * c
    chan = lax.broadcasted_iota(jnp.int32, (CHANS, LANES), 0)
    spread_ref[...] = jnp.where(chan == jnp.where(j < 6, base + j, -1), 1.0, 0.0).astype(BF)


def activated(values, gain):
    square_mean = jnp.mean(values * values, axis=-1, keepdims=True)
    normed = values * lax.rsqrt(square_mean + 1e-06) * gain
    return normed * jax.nn.sigmoid(normed)


def lay_out(active, spread_ref, out_ref):
    count = active.shape[0]
    laid = jnp.dot(active.astype(BF), spread_ref[...], preferred_element_type=F32)
    one = pltpu.roll(laid, count - 1, 0)
    out_ref[0, 0] = laid.astype(BF)
    out_ref[1, 0] = one.astype(BF)
    out_ref[2, 0] = pltpu.roll(laid, count - 2, 0).astype(BF)
    last = (lax.broadcasted_iota(jnp.int32, (count, 128), 1) & 7) >= 6
    for k in range(3):
        for part in (slice(0, 128), slice(128, 256)):
            pair = pltpu.roll(one[:, part], 6 - 2 * k, 1)
            out_ref[3 + k, 0, :, part] = jnp.where(last, pair, 0.0).astype(BF)


def first_layout_kernel(x_ref, gain_ref, out_ref, spread_ref):
    @pl.when(pl.program_id(0) == 0)
    def _():
        spread(spread_ref)

    values = x_ref[0].astype(F32).reshape(12 * 24, CHANS)
    lay_out(activated(values, gain_ref[...]), spread_ref, out_ref)


def first_layout(features, gain):
    return pl.pallas_call(
        first_layout_kernel,
        grid=(8,),
        out_shape=jax.ShapeDtypeStruct((6, 8, 12 * 24, LANES), BF),
        in_specs=[
            pl.BlockSpec((1, 12, 24, CHANS), lambda f: (f, 0, 0, 0)),
            pl.BlockSpec((1, CHANS), lambda f: (0, 0)),
        ],
        out_specs=pl.BlockSpec((6, 1, 12 * 24, LANES), lambda f: (0, f, 0, 0)),
        scratch_shapes=[pltpu.VMEM((CHANS, LANES), BF)],
        compiler_params=VMEM,
        name="first_layout",
    )(features, gain)


def second_layout_kernel(mine_ref, other_ref, bias_ref, gain_ref, out_ref, spread_ref):
    @pl.when(pl.program_id(0) == 0)
    def _():
        spread(spread_ref)

    t, h, z = (lax.axis_index(a) for a in AXES[:3])
    frame = pl.program_id(0) - 2 + 4 * t
    total = mine_ref[0] + other_ref[0].astype(F32) + bias_ref[...]
    active = activated(total.astype(BF).astype(F32), gain_ref[...])
    row = lax.broadcasted_iota(jnp.int32, (10, 24, 1), 0) + 8 * h - 1
    col = lax.broadcasted_iota(jnp.int32, (10, 24, 1), 1) + 20 * z - 1
    inside = (row >= 0) & (row < 32) & (col >= 0) & (col < 160) & (frame >= 0)
    active = active.reshape(10, 24, CHANS) * jnp.where(inside, 1.0, 0.0)
    lay_out(active.reshape(10 * 24, CHANS), spread_ref, out_ref)


def second_layout(mine, other, bias, gain):
    return pl.pallas_call(
        second_layout_kernel,
        grid=(6,),
        out_shape=jax.ShapeDtypeStruct((6, 6, 10 * 24, LANES), BF),
        in_specs=[
            pl.BlockSpec((1, 10 * 24, CHANS), lambda f: (f, 0, 0)),
            pl.BlockSpec((1, 10 * 24, CHANS), lambda f: (f, 0, 0)),
            pl.BlockSpec((1, CHANS), lambda f: (0, 0)),
            pl.BlockSpec((1, CHANS), lambda f: (0, 0)),
        ],
        out_specs=pl.BlockSpec((6, 1, 10 * 24, LANES), lambda f: (0, f, 0, 0)),
        scratch_shapes=[pltpu.VMEM((CHANS, LANES), BF)],
        compiler_params=VMEM,
        name="second_layout",
    )(mine, other, bias, gain)


def left_of(laid_ref, g, first, frames, count, lanes):
    def window(slot, tap):
        dt, start = tap // 9, 24 * (tap % 9 // 3)
        at = slice(start, start + count)
        return jnp.concatenate(
            [laid_ref[slot, first + dt + i, at, lanes] for i in range(frames)], axis=0
        )

    if g < len(MAIN):
        return window(MAIN[g] % 3, MAIN[g]) + window(3 + g % 3, PAIRED[g // 3])
    return window(1, ALONE[g - len(MAIN)])


def near_sum(laid_ref, blocks, first, frames, count):
    zeros = jnp.zeros((LANES // 4, CHANS), BF)
    total = None
    for g in range(GROUPS):
        rows = [b[i, g] for b in blocks for i in range(2)]
        right = jnp.concatenate(rows[:8] + [zeros] + rows[8:], axis=0)
        left = left_of(laid_ref, g, first, frames, count, slice(0, LANES))
        term = jnp.dot(left, right, preferred_element_type=F32)
        total = term if total is None else total + term
    return total


def far_sum(laid_ref, blocks, first, frames, count):
    total = None
    for base in range(0, GROUPS, 4):
        groups = range(base, min(base + 4, GROUPS))
        left, right = [], []
        for g in groups:
            left.append(left_of(laid_ref, g, first, frames, count, slice(128, 256))[:, :64])
            right += [b[i, g] for b in blocks for i in range(2)]
        left, right = jnp.concatenate(left, axis=1), jnp.concatenate(right, axis=0)
        term = jnp.dot(left, right, preferred_element_type=F32)
        total = term if total is None else total + term
    return total


def near_kernel(frames, count, laid_ref, *refs):
    *blocks, out_ref = refs
    total = near_sum(laid_ref, blocks, 2 * pl.program_id(0), 2, count)
    out_ref[...] = total.reshape(2, count, CHANS)


def near_conv(laid, blocks, frames, count):
    return pl.pallas_call(
        functools.partial(near_kernel, frames, count),
        grid=(frames // 2,),
        out_shape=jax.ShapeDtypeStruct((frames, count, CHANS), F32),
        in_specs=[whole] * (1 + len(blocks)),
        out_specs=pl.BlockSpec((2, count, CHANS), lambda f: (f, 0, 0)),
        compiler_params=VMEM,
        name="near_conv",
    )(laid, *blocks)


def first_conv_kernel(laid_ref, b0, b1, near_ref, mine_ref, sent_ref):
    total = far_sum(laid_ref, (b0, b1), 2 * pl.program_id(0), 2, 10 * 24)
    total = near_ref[...] + total.reshape(2, 10 * 24, CHANS)
    mine_ref[...] = total
    sent_ref[...] = total.astype(BF)


def first_conv(laid, blocks, near):
    out = pl.BlockSpec((2, 10 * 24, CHANS), lambda f: (f, 0, 0))
    return pl.pallas_call(
        first_conv_kernel,
        grid=(3,),
        out_shape=(
            jax.ShapeDtypeStruct((6, 10 * 24, CHANS), F32),
            jax.ShapeDtypeStruct((6, 10 * 24, CHANS), BF),
        ),
        in_specs=[whole] * 3 + [out],
        out_specs=(out, out),
        compiler_params=VMEM,
        name="first_conv",
    )(laid, *blocks, near)


def second_conv_kernel(laid_ref, b0, b1, near_ref, mine_ref, sent_ref, total_ref):
    total = far_sum(laid_ref, (b0, b1), 2 * pl.program_id(0), 2, 8 * 24)
    total = near_ref[...].reshape(2 * 192, CHANS) + total
    for part in range(3):
        total_ref[part] = total[:, 128 * part : 128 * part + 128]
    own = 10 * lax.axis_index("c")
    for f in range(2):
        for w in range(10):
            at = 192 * f + w
            mine_ref[f, w] = take(total_ref, at + own, 8, 24)
            sent_ref[f, w] = take(total_ref, at + 10 - own, 8, 24)


def second_conv(laid, blocks, near):
    out = pl.BlockSpec((2, 10, 8, CHANS), lambda f: (f, 0, 0, 0))
    return pl.pallas_call(
        second_conv_kernel,
        grid=(2,),
        out_shape=(
            jax.ShapeDtypeStruct((4, 10, 8, CHANS), F32),
            jax.ShapeDtypeStruct((4, 10, 8, CHANS), F32),
        ),
        in_specs=[whole] * 3 + [pl.BlockSpec((2, 8 * 24, CHANS), lambda f: (f, 0, 0))],
        out_specs=(out, out),
        scratch_shapes=[pltpu.VMEM((3, 2 * 192, 128), F32)],
        compiler_params=VMEM,
        name="second_conv",
    )(laid, *blocks, near)


def solution(mesh):
    sizes = (mesh.shape["tm"], mesh.shape["height"], mesh.shape["width"] // 2, 2)
    split = Mesh(mesh.devices.reshape(sizes), AXES)

    def sent(x, source):
        return move(x, sizes, source)

    def along(first, step):
        def source(t, h, z, c):
            return (t + step, h, z, c) if (c == 0) == first else (t, h + step, z, c)

        return source

    def z_near(x):
        return sent(x, lambda t, h, z, c: (t, h, z + SHIFT[c][t], c))

    def z_far(x):
        return sent(x, lambda t, h, z, c: (t, h, z + SHIFT[c][t] + 4, c))

    def two_planes_on(t, h, z, c):
        return (t, h, z + (-1, 1, 1, -1)[t], c) if c == 0 else (t, h + 2, z, c)

    def first_ring(x):
        up, down = sent(x, along(True, 1)), sent(x, along(True, -1))
        far = sent(x, two_planes_on)
        return [(jnp.stack([x[i], up[i]]), jnp.stack([far[i], down[i]])) for i in range(2)]

    def second_ring(x):
        return sent(x[0], along(False, 1)), sent(x[1], along(False, -1))

    def second_ring_rest(x):
        return sent(x[1], along(False, 1)), sent(x[0], along(False, -1))

    def passed_on(first_up, last_down):
        return sent(first_up, along(False, 1)), sent(last_down, along(False, -1))

    def in_order(x, first_up, last_down, last_up, first_down):
        return (*x, first_up, last_up, first_down, last_down)

    def swapped(x):
        return sent(x, lambda t, h, z, c: (t, h, z, 1 - c))

    def inner(at, d):
        return at if all(0 <= a < s for a, s in zip(at, sizes)) else None

    def taller(x):
        earlier = sent(x, lambda t, h, z, c: inner((t - 1, h, z, c), 0))
        return jnp.concatenate([earlier, x], axis=0)

    def higher(x):
        above = sent(x[:, -2:], lambda t, h, z, c: inner((t, h - 1, z, c), 0))
        below = sent(x[:, :2], lambda t, h, z, c: inner((t, h + 1, z, c), 0))
        return jnp.concatenate([above, x, below], axis=1)

    def wider(x, core):
        edge = jnp.where(core == 0, x[:, :, :2], x[:, :, -2:])
        beside = sent(edge, lambda t, h, z, c: inner((t, h, z + 2 * c - 1, 1 - c), 0))
        return jnp.where(
            core == 0,
            jnp.concatenate([beside, x], axis=2),
            jnp.concatenate([x, beside], axis=2),
        )

    def joined(mine, core):
        other = swapped(mine)
        return jnp.where(
            core == 0,
            jnp.concatenate([mine, other], axis=2),
            jnp.concatenate([other, mine], axis=2),
        )

    def at_once(*values):
        return lax.optimization_barrier(values)

    def on_device(features, gain_1, kernel_1, bias_1, gain_2, kernel_2, bias_2):
        core = lax.axis_index("c")
        gains = [v.reshape(1, CHANS) for v in (gain_1, gain_2, bias_1)]
        both = fold(kernel_1, kernel_2)
        both = jnp.concatenate([z_near(both), z_far(both)], axis=2)
        both, wide = at_once(both, higher(taller(features)))
        one, two = first_ring(both)
        (one, two), wide = at_once((one, two), joined(wider(wide, core), core))
        ends, rest = second_ring(one), second_ring_rest(one)
        ends, laid, two = at_once(ends, first_layout(wide, gains[0]), two)
        far = passed_on(*ends)
        next_ends = second_ring(two)
        near = near_conv(laid, in_order(one, *ends, *at_once(*rest)), 6, 10 * 24)
        far, near, next_ends = at_once(far, near, next_ends)
        mine, passed = first_conv(laid, far, near)
        next_rest = second_ring_rest(two)
        far = passed_on(*next_ends)
        laid = second_layout(mine, swapped(passed), gains[2], gains[1])
        near = near_conv(laid, in_order(two, *next_ends, *next_rest), 4, 8 * 24)
        mine, passed = second_conv(laid, far, near)
        own = jnp.transpose(features, (0, 2, 1, 3)).astype(F32)
        total = mine + swapped(passed) + bias_2 + own
        return jnp.transpose(total.astype(BF), (0, 2, 1, 3))

    volume = P("t", "h", ("z", "c"), None)
    weights = P(None, ("h", "z", "c"), None)
    return jax.shard_map(
        on_device,
        mesh=split,
        in_specs=(volume, P(), weights, P(), P(), weights, P()),
        out_specs=volume,
        check_vma=False,
    )
```

```python
import functools

import jax
import jax.numpy as jnp
from jax import lax
from jax.experimental import pallas as pl
from jax.experimental.pallas import tpu as pltpu
from jax.sharding import Mesh, PartitionSpec as P

AXES = ("t", "h", "z", "c")
SHIFT = ((0, 1, -1, 2), (0, -1, 1, 2))
MAIN = tuple(t for t in range(27) if t % 3 != 1)
PAIRED = (1, 4, 7, 10, 13, 16)
ALONE = (19, 22, 25)
GROUPS = len(MAIN) + len(ALONE)
CHANS = 384
LANES = 256
BF = jnp.bfloat16
F32 = jnp.float32
VMEM = pltpu.CompilerParams(vmem_limit_bytes=32 * 2**20)
whole = pl.BlockSpec(memory_space=pltpu.VMEM)


def move(x, sizes, source):
    def place(at):
        index = 0
        for coordinate, size in zip(at, sizes):
            index = index * size + coordinate % size
        return index

    pairs = []
    for index in range(sizes[0] * sizes[1] * sizes[2] * sizes[3]):
        rest, c = divmod(index, sizes[3])
        rest, z = divmod(rest, sizes[2])
        t, h = divmod(rest, sizes[1])
        at = source(t, h, z, c)
        if at is not None:
            pairs.append((place(at), index))
    return lax.ppermute(x, AXES, pairs)


def take(rows_ref, start, count, stride):
    return jnp.concatenate(
        [rows_ref[part, pl.ds(start, count, stride=stride)] for part in range(3)], axis=1
    )


def fold_kernel(k1_ref, k2_ref, out_ref, rows_ref):
    for which, k_ref in enumerate((k1_ref, k2_ref)):
        for r in range(6):
            for part in range(3):
                values = k_ref[r, :, 128 * part : 128 * part + 128]
                rows_ref[part, 32 * r : 32 * r + 27] = values.astype(F32)
        for g in range(GROUPS):
            if g < len(MAIN):
                low = take(rows_ref, MAIN[g], 6, 32)
                high = take(rows_ref, 64 * (g % 3) + PAIRED[g // 3], 2, 32)
            else:
                low = take(rows_ref, ALONE[g - len(MAIN)], 6, 32)
                high = jnp.zeros((2, CHANS), F32)
            out_ref[which, g] = jnp.concatenate([low, high], axis=0).astype(BF)


def fold(kernel_1, kernel_2):
    return pl.pallas_call(
        fold_kernel,
        out_shape=jax.ShapeDtypeStruct((2, GROUPS, 8, CHANS), BF),
        in_specs=[whole] * 2,
        out_specs=whole,
        scratch_shapes=[pltpu.VMEM((3, 192, 128), F32)],
        compiler_params=VMEM,
        name="fold",
    )(jnp.transpose(kernel_1, (1, 0, 2)), jnp.transpose(kernel_2, (1, 0, 2)))


def spread(spread_ref):
    t, h, z, c = (lax.axis_index(a) for a in AXES)
    lane = lax.broadcasted_iota(jnp.int32, (1, LANES), 1)
    j = lane & 7
    p = lane >> 3
    outer, inner, far = p >> 3, (p >> 1) & 3, p & 1
    t_of = (t + jnp.where(c == 0, inner, outer)) & 3
    h_of = (h + jnp.where(c == 0, outer, inner)) & 3
    sides = jnp.where((t_of == 1) == (c == 0), 1, 7)
    shift = jnp.where(t_of == 0, 0, jnp.where(t_of == 3, 2, sides))
    z_of = (z + shift + 4 * far) & 7
    base = 96 * h_of + 12 * z_of + 6 * c
    chan = lax.broadcasted_iota(jnp.int32, (CHANS, LANES), 0)
    spread_ref[...] = jnp.where(chan == jnp.where(j < 6, base + j, -1), 1.0, 0.0).astype(BF)


def activated(values, gain):
    square_mean = jnp.mean(values * values, axis=-1, keepdims=True)
    normed = values * lax.rsqrt(square_mean + 1e-06) * gain
    return normed * jax.nn.sigmoid(normed)


def lay_out(active, spread_ref, out_ref):
    count = active.shape[0]
    laid = jnp.dot(active.astype(BF), spread_ref[...], preferred_element_type=F32)
    one = pltpu.roll(laid, count - 1, 0)
    out_ref[0, 0] = laid.astype(BF)
    out_ref[1, 0] = one.astype(BF)
    out_ref[2, 0] = pltpu.roll(laid, count - 2, 0).astype(BF)
    last = (lax.broadcasted_iota(jnp.int32, (count, 128), 1) & 7) >= 6
    for k in range(3):
        for part in (slice(0, 128), slice(128, 256)):
            pair = pltpu.roll(one[:, part], 6 - 2 * k, 1)
            out_ref[3 + k, 0, :, part] = jnp.where(last, pair, 0.0).astype(BF)


def first_layout_kernel(x_ref, gain_ref, out_ref, spread_ref):
    @pl.when(pl.program_id(0) == 0)
    def _():
        spread(spread_ref)

    values = x_ref[0].astype(F32).reshape(12 * 24, CHANS)
    lay_out(activated(values, gain_ref[...]), spread_ref, out_ref)


def first_layout(features, gain):
    return pl.pallas_call(
        first_layout_kernel,
        grid=(8,),
        out_shape=jax.ShapeDtypeStruct((6, 8, 12 * 24, LANES), BF),
        in_specs=[
            pl.BlockSpec((1, 12, 24, CHANS), lambda f: (f, 0, 0, 0)),
            pl.BlockSpec((1, CHANS), lambda f: (0, 0)),
        ],
        out_specs=pl.BlockSpec((6, 1, 12 * 24, LANES), lambda f: (0, f, 0, 0)),
        scratch_shapes=[pltpu.VMEM((CHANS, LANES), BF)],
        compiler_params=VMEM,
        name="first_layout",
    )(features, gain)


def second_layout_kernel(mine_ref, other_ref, bias_ref, gain_ref, out_ref, spread_ref):
    @pl.when(pl.program_id(0) == 0)
    def _():
        spread(spread_ref)

    t, h, z = (lax.axis_index(a) for a in AXES[:3])
    frame = pl.program_id(0) - 2 + 4 * t
    total = mine_ref[0] + other_ref[0].astype(F32) + bias_ref[...]
    active = activated(total.astype(BF).astype(F32), gain_ref[...])
    row = lax.broadcasted_iota(jnp.int32, (10, 24, 1), 0) + 8 * h - 1
    col = lax.broadcasted_iota(jnp.int32, (10, 24, 1), 1) + 20 * z - 1
    inside = (row >= 0) & (row < 32) & (col >= 0) & (col < 160) & (frame >= 0)
    active = active.reshape(10, 24, CHANS) * jnp.where(inside, 1.0, 0.0)
    lay_out(active.reshape(10 * 24, CHANS), spread_ref, out_ref)


def second_layout(mine, other, bias, gain):
    return pl.pallas_call(
        second_layout_kernel,
        grid=(6,),
        out_shape=jax.ShapeDtypeStruct((6, 6, 10 * 24, LANES), BF),
        in_specs=[
            pl.BlockSpec((1, 10 * 24, CHANS), lambda f: (f, 0, 0)),
            pl.BlockSpec((1, 10 * 24, CHANS), lambda f: (f, 0, 0)),
            pl.BlockSpec((1, CHANS), lambda f: (0, 0)),
            pl.BlockSpec((1, CHANS), lambda f: (0, 0)),
        ],
        out_specs=pl.BlockSpec((6, 1, 10 * 24, LANES), lambda f: (0, f, 0, 0)),
        scratch_shapes=[pltpu.VMEM((CHANS, LANES), BF)],
        compiler_params=VMEM,
        name="second_layout",
    )(mine, other, bias, gain)


def left_of(laid_ref, g, first, frames, count, lanes):
    def window(slot, tap):
        dt, start = tap // 9, 24 * (tap % 9 // 3)
        at = slice(start, start + count)
        return jnp.concatenate(
            [laid_ref[slot, first + dt + i, at, lanes] for i in range(frames)], axis=0
        )

    if g < len(MAIN):
        return window(MAIN[g] % 3, MAIN[g]) + window(3 + g % 3, PAIRED[g // 3])
    return window(1, ALONE[g - len(MAIN)])


def near_sum(laid_ref, blocks, first, frames, count):
    zeros = jnp.zeros((LANES // 4, CHANS), BF)
    total = None
    for g in range(GROUPS):
        rows = [b[i, g] for b in blocks for i in range(2)]
        right = jnp.concatenate(rows[:8] + [zeros] + rows[8:], axis=0)
        left = left_of(laid_ref, g, first, frames, count, slice(0, LANES))
        term = jnp.dot(left, right, preferred_element_type=F32)
        total = term if total is None else total + term
    return total


def far_sum(laid_ref, blocks, first, frames, count):
    total = None
    for base in range(0, GROUPS, 4):
        groups = range(base, min(base + 4, GROUPS))
        left, right = [], []
        for g in groups:
            left.append(left_of(laid_ref, g, first, frames, count, slice(128, 256))[:, :64])
            right += [b[i, g] for b in blocks for i in range(2)]
        left, right = jnp.concatenate(left, axis=1), jnp.concatenate(right, axis=0)
        term = jnp.dot(left, right, preferred_element_type=F32)
        total = term if total is None else total + term
    return total


def near_kernel(frames, count, laid_ref, *refs):
    *blocks, out_ref = refs
    total = near_sum(laid_ref, blocks, 2 * pl.program_id(0), 2, count)
    out_ref[...] = total.reshape(2, count, CHANS)


def near_conv(laid, blocks, frames, count):
    return pl.pallas_call(
        functools.partial(near_kernel, frames, count),
        grid=(frames // 2,),
        out_shape=jax.ShapeDtypeStruct((frames, count, CHANS), F32),
        in_specs=[whole] * (1 + len(blocks)),
        out_specs=pl.BlockSpec((2, count, CHANS), lambda f: (f, 0, 0)),
        compiler_params=VMEM,
        name="near_conv",
    )(laid, *blocks)


def first_conv_kernel(laid_ref, b0, b1, near_ref, mine_ref, sent_ref):
    total = far_sum(laid_ref, (b0, b1), 2 * pl.program_id(0), 2, 10 * 24)
    total = near_ref[...] + total.reshape(2, 10 * 24, CHANS)
    mine_ref[...] = total
    sent_ref[...] = total.astype(BF)


def first_conv(laid, blocks, near):
    out = pl.BlockSpec((2, 10 * 24, CHANS), lambda f: (f, 0, 0))
    return pl.pallas_call(
        first_conv_kernel,
        grid=(3,),
        out_shape=(
            jax.ShapeDtypeStruct((6, 10 * 24, CHANS), F32),
            jax.ShapeDtypeStruct((6, 10 * 24, CHANS), BF),
        ),
        in_specs=[whole] * 3 + [out],
        out_specs=(out, out),
        compiler_params=VMEM,
        name="first_conv",
    )(laid, *blocks, near)


def second_conv_kernel(laid_ref, b0, b1, near_ref, mine_ref, sent_ref, total_ref):
    total = far_sum(laid_ref, (b0, b1), 2 * pl.program_id(0), 2, 8 * 24)
    total = near_ref[...].reshape(2 * 192, CHANS) + total
    for part in range(3):
        total_ref[part] = total[:, 128 * part : 128 * part + 128]
    own = 10 * lax.axis_index("c")
    for f in range(2):
        for w in range(10):
            at = 192 * f + w
            mine_ref[f, w] = take(total_ref, at + own, 8, 24)
            sent_ref[f, w] = take(total_ref, at + 10 - own, 8, 24)


def second_conv(laid, blocks, near):
    out = pl.BlockSpec((2, 10, 8, CHANS), lambda f: (f, 0, 0, 0))
    return pl.pallas_call(
        second_conv_kernel,
        grid=(2,),
        out_shape=(
            jax.ShapeDtypeStruct((4, 10, 8, CHANS), F32),
            jax.ShapeDtypeStruct((4, 10, 8, CHANS), F32),
        ),
        in_specs=[whole] * 3 + [pl.BlockSpec((2, 8 * 24, CHANS), lambda f: (f, 0, 0))],
        out_specs=(out, out),
        scratch_shapes=[pltpu.VMEM((3, 2 * 192, 128), F32)],
        compiler_params=VMEM,
        name="second_conv",
    )(laid, *blocks, near)


def solution(mesh):
    sizes = (mesh.shape["tm"], mesh.shape["height"], mesh.shape["width"] // 2, 2)
    split = Mesh(mesh.devices.reshape(sizes), AXES)

    def sent(x, source):
        return move(x, sizes, source)

    def along(first, step):
        def source(t, h, z, c):
            return (t + step, h, z, c) if (c == 0) == first else (t, h + step, z, c)

        return source

    def z_near(x):
        return sent(x, lambda t, h, z, c: (t, h, z + SHIFT[c][t], c))

    def z_far(x):
        return sent(x, lambda t, h, z, c: (t, h, z + SHIFT[c][t] + 4, c))

    def two_planes_on(t, h, z, c):
        return (t, h, z + (-1, 1, 1, -1)[t], c) if c == 0 else (t, h + 2, z, c)

    def first_ring(x):
        up, down = sent(x, along(True, 1)), sent(x, along(True, -1))
        far = sent(x, two_planes_on)
        return [(jnp.stack([x[i], up[i]]), jnp.stack([far[i], down[i]])) for i in range(2)]

    def second_ring(x):
        return sent(x[0], along(False, 1)), sent(x[1], along(False, -1))

    def second_ring_rest(x):
        return sent(x[1], along(False, 1)), sent(x[0], along(False, -1))

    def passed_on(first_up, last_down):
        return sent(first_up, along(False, 1)), sent(last_down, along(False, -1))

    def in_order(x, first_up, last_down, last_up, first_down):
        return (*x, first_up, last_up, first_down, last_down)

    def swapped(x):
        return sent(x, lambda t, h, z, c: (t, h, z, 1 - c))

    def inner(at, d):
        return at if all(0 <= a < s for a, s in zip(at, sizes)) else None

    def taller(x):
        earlier = sent(x, lambda t, h, z, c: inner((t - 1, h, z, c), 0))
        return jnp.concatenate([earlier, x], axis=0)

    def higher(x):
        above = sent(x[:, -2:], lambda t, h, z, c: inner((t, h - 1, z, c), 0))
        below = sent(x[:, :2], lambda t, h, z, c: inner((t, h + 1, z, c), 0))
        return jnp.concatenate([above, x, below], axis=1)

    def wider(x, core):
        edge = jnp.where(core == 0, x[:, :, :2], x[:, :, -2:])
        beside = sent(edge, lambda t, h, z, c: inner((t, h, z + 2 * c - 1, 1 - c), 0))
        return jnp.where(
            core == 0,
            jnp.concatenate([beside, x], axis=2),
            jnp.concatenate([x, beside], axis=2),
        )

    def joined(mine, other, core):
        return jnp.where(
            core == 0,
            jnp.concatenate([mine, other], axis=2),
            jnp.concatenate([other, mine], axis=2),
        )

    def at_once(*values):
        return lax.optimization_barrier(values)

    def on_device(features, gain_1, kernel_1, bias_1, gain_2, kernel_2, bias_2):
        core = lax.axis_index("c")
        gains = [v.reshape(1, CHANS) for v in (gain_1, gain_2, bias_1)]
        both = fold(kernel_1, kernel_2)
        both = jnp.concatenate([z_near(both), z_far(both)], axis=2)
        both, wide = at_once(both, higher(taller(features)))
        one, two = first_ring(both)
        wide = wider(wide, core)
        (one, two), wide, other = at_once((one, two), wide, swapped(wide))
        wide = joined(wide, other, core)
        ends, rest = second_ring(one), second_ring_rest(one)
        ends, laid, two = at_once(ends, first_layout(wide, gains[0]), two)
        far = passed_on(*ends)
        next_ends = second_ring(two)
        near = near_conv(laid, in_order(one, *ends, *at_once(*rest)), 6, 10 * 24)
        far, near, next_ends = at_once(far, near, next_ends)
        mine, passed = first_conv(laid, far, near)
        next_rest = second_ring_rest(two)
        far = passed_on(*next_ends)
        laid = second_layout(mine, swapped(passed), gains[2], gains[1])
        near = near_conv(laid, in_order(two, *next_ends, *next_rest), 4, 8 * 24)
        mine, passed = second_conv(laid, far, near)
        own = jnp.transpose(features, (0, 2, 1, 3)).astype(F32)
        total = mine + swapped(passed) + bias_2 + own
        return jnp.transpose(total.astype(BF), (0, 2, 1, 3))

    volume = P("t", "h", ("z", "c"), None)
    weights = P(None, ("h", "z", "c"), None)
    return jax.shard_map(
        on_device,
        mesh=split,
        in_specs=(volume, P(), weights, P(), P(), weights, P()),
        out_specs=volume,
        check_vma=False,
    )
```

```python
import functools

import jax
import jax.numpy as jnp
from jax import lax
from jax.experimental import pallas as pl
from jax.experimental.pallas import tpu as pltpu
from jax.sharding import Mesh, PartitionSpec as P

AXES = ("t", "h", "z", "c")
SHIFT = ((0, 1, -1, 2), (0, -1, 1, 2))
MAIN = tuple(t for t in range(27) if t % 3 != 1)
PAIRED = (1, 4, 7, 10, 13, 16)
ALONE = (19, 22, 25)
GROUPS = len(MAIN) + len(ALONE)
CHANS = 384
LANES = 256
BF = jnp.bfloat16
F32 = jnp.float32
VMEM = pltpu.CompilerParams(vmem_limit_bytes=32 * 2**20)
whole = pl.BlockSpec(memory_space=pltpu.VMEM)


def move(x, sizes, source):
    def place(at):
        index = 0
        for coordinate, size in zip(at, sizes):
            index = index * size + coordinate % size
        return index

    pairs = []
    for index in range(sizes[0] * sizes[1] * sizes[2] * sizes[3]):
        rest, c = divmod(index, sizes[3])
        rest, z = divmod(rest, sizes[2])
        t, h = divmod(rest, sizes[1])
        at = source(t, h, z, c)
        if at is not None:
            pairs.append((place(at), index))
    return lax.ppermute(x, AXES, pairs)


def take(rows_ref, start, count, stride):
    return jnp.concatenate(
        [rows_ref[part, pl.ds(start, count, stride=stride)] for part in range(3)], axis=1
    )


def fold_kernel(k1_ref, k2_ref, out_ref, rows_ref):
    for which, k_ref in enumerate((k1_ref, k2_ref)):
        for r in range(6):
            for part in range(3):
                values = k_ref[r, :, 128 * part : 128 * part + 128]
                rows_ref[part, 32 * r : 32 * r + 27] = values.astype(F32)
        for g in range(GROUPS):
            if g < len(MAIN):
                low = take(rows_ref, MAIN[g], 6, 32)
                high = take(rows_ref, 64 * (g % 3) + PAIRED[g // 3], 2, 32)
            else:
                low = take(rows_ref, ALONE[g - len(MAIN)], 6, 32)
                high = jnp.zeros((2, CHANS), F32)
            out_ref[which, g] = jnp.concatenate([low, high], axis=0).astype(BF)


def fold(kernel_1, kernel_2):
    return pl.pallas_call(
        fold_kernel,
        out_shape=jax.ShapeDtypeStruct((2, GROUPS, 8, CHANS), BF),
        in_specs=[whole] * 2,
        out_specs=whole,
        scratch_shapes=[pltpu.VMEM((3, 192, 128), F32)],
        compiler_params=VMEM,
        name="fold",
    )(jnp.transpose(kernel_1, (1, 0, 2)), jnp.transpose(kernel_2, (1, 0, 2)))


def spread(spread_ref):
    t, h, z, c = (lax.axis_index(a) for a in AXES)
    lane = lax.broadcasted_iota(jnp.int32, (1, LANES), 1)
    j = lane & 7
    p = lane >> 3
    outer, inner, far = p >> 3, (p >> 1) & 3, p & 1
    t_of = (t + jnp.where(c == 0, inner, outer)) & 3
    h_of = (h + jnp.where(c == 0, outer, inner)) & 3
    sides = jnp.where((t_of == 1) == (c == 0), 1, 7)
    shift = jnp.where(t_of == 0, 0, jnp.where(t_of == 3, 2, sides))
    z_of = (z + shift + 4 * far) & 7
    base = 96 * h_of + 12 * z_of + 6 * c
    chan = lax.broadcasted_iota(jnp.int32, (CHANS, LANES), 0)
    spread_ref[...] = jnp.where(chan == jnp.where(j < 6, base + j, -1), 1.0, 0.0).astype(BF)


def activated(values, gain):
    square_mean = jnp.mean(values * values, axis=-1, keepdims=True)
    normed = values * lax.rsqrt(square_mean + 1e-06) * gain
    return normed * jax.nn.sigmoid(normed)


def lay_out(active, spread_ref, out_ref):
    count = active.shape[0]
    laid = jnp.dot(active.astype(BF), spread_ref[...], preferred_element_type=F32)
    one = pltpu.roll(laid, count - 1, 0)
    out_ref[0, 0] = laid.astype(BF)
    out_ref[1, 0] = one.astype(BF)
    out_ref[2, 0] = pltpu.roll(laid, count - 2, 0).astype(BF)
    last = (lax.broadcasted_iota(jnp.int32, (count, 128), 1) & 7) >= 6
    for k in range(3):
        for part in (slice(0, 128), slice(128, 256)):
            pair = pltpu.roll(one[:, part], 6 - 2 * k, 1)
            out_ref[3 + k, 0, :, part] = jnp.where(last, pair, 0.0).astype(BF)


def first_layout_kernel(x_ref, gain_ref, out_ref, spread_ref):
    @pl.when(pl.program_id(0) == 0)
    def _():
        spread(spread_ref)

    values = x_ref[0].astype(F32).reshape(12 * 24, CHANS)
    lay_out(activated(values, gain_ref[...]), spread_ref, out_ref)


def first_layout(features, gain):
    return pl.pallas_call(
        first_layout_kernel,
        grid=(8,),
        out_shape=jax.ShapeDtypeStruct((6, 8, 12 * 24, LANES), BF),
        in_specs=[
            pl.BlockSpec((1, 12, 24, CHANS), lambda f: (f, 0, 0, 0)),
            pl.BlockSpec((1, CHANS), lambda f: (0, 0)),
        ],
        out_specs=pl.BlockSpec((6, 1, 12 * 24, LANES), lambda f: (0, f, 0, 0)),
        scratch_shapes=[pltpu.VMEM((CHANS, LANES), BF)],
        compiler_params=VMEM,
        name="first_layout",
    )(features, gain)


def second_layout_kernel(mine_ref, other_ref, bias_ref, gain_ref, out_ref, spread_ref):
    @pl.when(pl.program_id(0) == 0)
    def _():
        spread(spread_ref)

    t, h, z = (lax.axis_index(a) for a in AXES[:3])
    frame = pl.program_id(0) - 2 + 4 * t
    total = mine_ref[0] + other_ref[0].astype(F32) + bias_ref[...]
    active = activated(total.astype(BF).astype(F32), gain_ref[...])
    row = lax.broadcasted_iota(jnp.int32, (10, 24, 1), 0) + 8 * h - 1
    col = lax.broadcasted_iota(jnp.int32, (10, 24, 1), 1) + 20 * z - 1
    inside = (row >= 0) & (row < 32) & (col >= 0) & (col < 160) & (frame >= 0)
    active = active.reshape(10, 24, CHANS) * jnp.where(inside, 1.0, 0.0)
    lay_out(active.reshape(10 * 24, CHANS), spread_ref, out_ref)


def second_layout(mine, other, bias, gain):
    return pl.pallas_call(
        second_layout_kernel,
        grid=(6,),
        out_shape=jax.ShapeDtypeStruct((6, 6, 10 * 24, LANES), BF),
        in_specs=[
            pl.BlockSpec((1, 10 * 24, CHANS), lambda f: (f, 0, 0)),
            pl.BlockSpec((1, 10 * 24, CHANS), lambda f: (f, 0, 0)),
            pl.BlockSpec((1, CHANS), lambda f: (0, 0)),
            pl.BlockSpec((1, CHANS), lambda f: (0, 0)),
        ],
        out_specs=pl.BlockSpec((6, 1, 10 * 24, LANES), lambda f: (0, f, 0, 0)),
        scratch_shapes=[pltpu.VMEM((CHANS, LANES), BF)],
        compiler_params=VMEM,
        name="second_layout",
    )(mine, other, bias, gain)


def left_of(laid_ref, g, first, frames, count, lanes):
    def window(slot, tap):
        dt, start = tap // 9, 24 * (tap % 9 // 3)
        at = slice(start, start + count)
        return jnp.concatenate(
            [laid_ref[slot, first + dt + i, at, lanes] for i in range(frames)], axis=0
        )

    if g < len(MAIN):
        return window(MAIN[g] % 3, MAIN[g]) + window(3 + g % 3, PAIRED[g // 3])
    return window(1, ALONE[g - len(MAIN)])


def near_sum(laid_ref, blocks, first, frames, count):
    zeros = jnp.zeros((LANES // 4, CHANS), BF)
    total = None
    for g in range(GROUPS):
        rows = [b[i, g] for b in blocks for i in range(2)]
        right = jnp.concatenate(rows[:8] + [zeros] + rows[8:], axis=0)
        left = left_of(laid_ref, g, first, frames, count, slice(0, LANES))
        term = jnp.dot(left, right, preferred_element_type=F32)
        total = term if total is None else total + term
    return total


def far_sum(laid_ref, blocks, first, frames, count):
    total = None
    for base in range(0, GROUPS, 4):
        groups = range(base, min(base + 4, GROUPS))
        left, right = [], []
        for g in groups:
            left.append(left_of(laid_ref, g, first, frames, count, slice(128, 256))[:, :64])
            right += [b[i, g] for b in blocks for i in range(2)]
        left, right = jnp.concatenate(left, axis=1), jnp.concatenate(right, axis=0)
        term = jnp.dot(left, right, preferred_element_type=F32)
        total = term if total is None else total + term
    return total


def near_kernel(frames, count, laid_ref, *refs):
    *blocks, out_ref = refs
    total = near_sum(laid_ref, blocks, 2 * pl.program_id(0), 2, count)
    out_ref[...] = total.reshape(2, count, CHANS)


def near_conv(laid, blocks, frames, count):
    return pl.pallas_call(
        functools.partial(near_kernel, frames, count),
        grid=(frames // 2,),
        out_shape=jax.ShapeDtypeStruct((frames, count, CHANS), F32),
        in_specs=[whole] * (1 + len(blocks)),
        out_specs=pl.BlockSpec((2, count, CHANS), lambda f: (f, 0, 0)),
        compiler_params=VMEM,
        name="near_conv",
    )(laid, *blocks)


def first_conv_kernel(laid_ref, b0, b1, near_ref, mine_ref, sent_ref):
    total = far_sum(laid_ref, (b0, b1), 2 * pl.program_id(0), 2, 10 * 24)
    total = near_ref[...] + total.reshape(2, 10 * 24, CHANS)
    mine_ref[...] = total
    sent_ref[...] = total.astype(BF)


def first_conv(laid, blocks, near):
    out = pl.BlockSpec((2, 10 * 24, CHANS), lambda f: (f, 0, 0))
    return pl.pallas_call(
        first_conv_kernel,
        grid=(3,),
        out_shape=(
            jax.ShapeDtypeStruct((6, 10 * 24, CHANS), F32),
            jax.ShapeDtypeStruct((6, 10 * 24, CHANS), BF),
        ),
        in_specs=[whole] * 3 + [out],
        out_specs=(out, out),
        compiler_params=VMEM,
        name="first_conv",
    )(laid, *blocks, near)


def second_conv_kernel(laid_ref, b0, b1, near_ref, mine_ref, sent_ref, total_ref):
    total = far_sum(laid_ref, (b0, b1), 2 * pl.program_id(0), 2, 8 * 24)
    total = near_ref[...].reshape(2 * 192, CHANS) + total
    for part in range(3):
        total_ref[part] = total[:, 128 * part : 128 * part + 128]
    own = 10 * lax.axis_index("c")
    for f in range(2):
        for w in range(10):
            at = 192 * f + w
            mine_ref[f, w] = take(total_ref, at + own, 8, 24)
            sent_ref[f, w] = take(total_ref, at + 10 - own, 8, 24).astype(BF)


def second_conv(laid, blocks, near):
    out = pl.BlockSpec((2, 10, 8, CHANS), lambda f: (f, 0, 0, 0))
    return pl.pallas_call(
        second_conv_kernel,
        grid=(2,),
        out_shape=(
            jax.ShapeDtypeStruct((4, 10, 8, CHANS), F32),
            jax.ShapeDtypeStruct((4, 10, 8, CHANS), BF),
        ),
        in_specs=[whole] * 3 + [pl.BlockSpec((2, 8 * 24, CHANS), lambda f: (f, 0, 0))],
        out_specs=(out, out),
        scratch_shapes=[pltpu.VMEM((3, 2 * 192, 128), F32)],
        compiler_params=VMEM,
        name="second_conv",
    )(laid, *blocks, near)


def solution(mesh):
    sizes = (mesh.shape["tm"], mesh.shape["height"], mesh.shape["width"] // 2, 2)
    split = Mesh(mesh.devices.reshape(sizes), AXES)

    def sent(x, source):
        return move(x, sizes, source)

    def along(first, step):
        def source(t, h, z, c):
            return (t + step, h, z, c) if (c == 0) == first else (t, h + step, z, c)

        return source

    def z_near(x):
        return sent(x, lambda t, h, z, c: (t, h, z + SHIFT[c][t], c))

    def z_far(x):
        return sent(x, lambda t, h, z, c: (t, h, z + SHIFT[c][t] + 4, c))

    def two_planes_on(t, h, z, c):
        return (t, h, z + (-1, 1, 1, -1)[t], c) if c == 0 else (t, h + 2, z, c)

    def first_ring(x):
        up, down = sent(x, along(True, 1)), sent(x, along(True, -1))
        far = sent(x, two_planes_on)
        return [(jnp.stack([x[i], up[i]]), jnp.stack([far[i], down[i]])) for i in range(2)]

    def second_ring(x):
        return sent(x[0], along(False, 1)), sent(x[1], along(False, -1))

    def second_ring_rest(x):
        return sent(x[1], along(False, 1)), sent(x[0], along(False, -1))

    def passed_on(first_up, last_down):
        return sent(first_up, along(False, 1)), sent(last_down, along(False, -1))

    def in_order(x, first_up, last_down, last_up, first_down):
        return (*x, first_up, last_up, first_down, last_down)

    def swapped(x):
        return sent(x, lambda t, h, z, c: (t, h, z, 1 - c))

    def inner(at, d):
        return at if all(0 <= a < s for a, s in zip(at, sizes)) else None

    def taller(x):
        earlier = sent(x, lambda t, h, z, c: inner((t - 1, h, z, c), 0))
        return jnp.concatenate([earlier, x], axis=0)

    def higher(x):
        above = sent(x[:, -2:], lambda t, h, z, c: inner((t, h - 1, z, c), 0))
        below = sent(x[:, :2], lambda t, h, z, c: inner((t, h + 1, z, c), 0))
        return jnp.concatenate([above, x, below], axis=1)

    def wider(x, core):
        edge = jnp.where(core == 0, x[:, :, :2], x[:, :, -2:])
        beside = sent(edge, lambda t, h, z, c: inner((t, h, z + 2 * c - 1, 1 - c), 0))
        return jnp.where(
            core == 0,
            jnp.concatenate([beside, x], axis=2),
            jnp.concatenate([x, beside], axis=2),
        )

    def joined(mine, other, core):
        return jnp.where(
            core == 0,
            jnp.concatenate([mine, other], axis=2),
            jnp.concatenate([other, mine], axis=2),
        )

    def at_once(*values):
        return lax.optimization_barrier(values)

    def on_device(features, gain_1, kernel_1, bias_1, gain_2, kernel_2, bias_2):
        core = lax.axis_index("c")
        gains = [v.reshape(1, CHANS) for v in (gain_1, gain_2, bias_1)]
        both = fold(kernel_1, kernel_2)
        both = jnp.concatenate([z_near(both), z_far(both)], axis=2)
        both, wide = at_once(both, higher(taller(features)))
        one, two = first_ring(both)
        wide = wider(wide, core)
        (one, two), wide, other = at_once((one, two), wide, swapped(wide))
        wide = joined(wide, other, core)
        ends, rest = second_ring(one), second_ring_rest(one)
        ends, laid, two = at_once(ends, first_layout(wide, gains[0]), two)
        far = passed_on(*ends)
        next_ends = second_ring(two)
        near = near_conv(laid, in_order(one, *ends, *at_once(*rest)), 6, 10 * 24)
        far, near, next_ends = at_once(far, near, next_ends)
        mine, passed = first_conv(laid, far, near)
        next_rest = second_ring_rest(two)
        far = passed_on(*next_ends)
        laid = second_layout(mine, swapped(passed), gains[2], gains[1])
        near = near_conv(laid, in_order(two, *next_ends, *next_rest), 4, 8 * 24)
        mine, passed = second_conv(laid, far, near)
        own = jnp.transpose(features, (0, 2, 1, 3)).astype(F32)
        total = mine + swapped(passed).astype(F32) + bias_2 + own
        return jnp.transpose(total.astype(BF), (0, 2, 1, 3))

    volume = P("t", "h", ("z", "c"), None)
    weights = P(None, ("h", "z", "c"), None)
    return jax.shard_map(
        on_device,
        mesh=split,
        in_specs=(volume, P(), weights, P(), P(), weights, P()),
        out_specs=volume,
        check_vma=False,
    )
```
